32 devices in a mesh: slab: 2 (over x), space: 8 (over z, y), elec: 2 (over core).
Axes of the slice: x: 2, y: 2, z: 4, core: 2. Of those that a mesh axis runs over, the one named last changes fastest.
Arguments:
- potentials: bfloat16 [1024, 32, 1024], P('elec', ('slab', 'space')), parts along dimension 1, may hold values from -6 to 6
- elec_order: int32 [1024], replicated, may hold values from 0 to 1023, each once
- quadripoles: int32 [1024, 4], replicated, may hold values from 0 to 1023, all different within a row
- weighted_misfit: bfloat16 [2048], P('slab'), parts along dimension 0, may hold values from -6 to 6
- salinity: float32 [32, 1024], P(('slab', 'space')), parts along dimension 0, may hold values from 1 to 35
- water_content: float32 [32, 1024], P(('slab', 'space')), parts along dimension 0, may hold values from 0.15 to 0.45
- cementation: float32 [32, 1024], P(('slab', 'space')), parts along dimension 0, may hold values from 1.3 to 2.5
- anisotropy: float32 [3, 32, 1024], P(None, ('slab', 'space')), parts along dimension 1, may hold values from 0.1 to 1.9
Outputs:
- grad_salt: float32 [32, 1024], P(('slab', 'space')), parts along dimension 0
- grad_water: float32 [32, 1024], P(('slab', 'space')), parts along dimension 0
The draws below stay inside these ranges and needn't reach their ends.
There are 2 independent parts, one for each index of `slab`. The reference program is written for one: setup_inputs(seed, part) draws one part's arguments, and reference() takes and returns one part's arrays. A program takes and returns all parts, laid end to end along the dimension named above; an argument that names none is the same for every part. Nothing has to cross between parts.
Inputs may be any that keep to these rules, and one draw needn't show every extreme that they name: `elec_order`: a permutation of the electrodes. `quadripoles`: the four electrodes of a measurement differ; every electrode takes part in some measurement.
All inputs are finite; a program needn't handle non-finite values.
Results may differ from the reference program's by a relative error of at most 0.0045.
Values may be sent and summed in bfloat16 or wider, within the bound.
No kernel may reach another device: no remote copies, remote signals or barrier semaphores. Data moves between devices by JAX's collectives and lax.ppermute only.
A program may use at most 64 MiB of HBM per device.

```python
import math
import jax
import jax.numpy as jnp
from jax import lax

ELECTRODE_COUNT = 1024
MEASURE_COUNT = 1024
NX = 32
NY = 32
CZ = 2
NZ = 16
NXY = 1024


def block_levels(rng, dims, cuts, least, largest):
    level, own = 1.0, jax.random.fold_in(rng, 6)
    for dim, shards_of in cuts:
        steps = jnp.exp(jax.random.uniform(jax.random.fold_in(own, dim), (shards_of,), jnp.float32, least / len(cuts), largest / len(cuts)))
        level = level * jnp.repeat(steps, dims[dim] // shards_of).reshape([-1 if axis == dim else 1 for axis in range(len(dims))])
    return level


def choose_distinct(stream_key, rows, amount, top, lift):
    order = jax.random.permutation(jax.random.fold_in(stream_key, 1), amount)
    favour = order
    for power in range(3):
        favour = favour * favour // amount
    favour = favour * lift // amount
    chance = jax.random.randint(jax.random.fold_in(stream_key, 2), (rows, amount), 0, 4096) + favour
    fixed_rows = jax.random.permutation(jax.random.fold_in(stream_key, 3), rows)[jnp.arange(amount) % rows]
    chance = jnp.where(jnp.arange(rows)[:, None] == fixed_rows[None, :], 1 << 14, chance)
    score = chance * amount + jnp.arange(amount)
    return lax.top_k(score.astype(jnp.int32), top)[1].astype(jnp.int32)


def scatter_about(key, extent, scale, reach, cuts=(), kind=jnp.bfloat16):
    gain = block_levels(key, extent, cuts, -0.22, 0.18) if cuts else 1.0
    array = jax.random.normal(key, extent, jnp.float32) * scale * gain
    return jnp.minimum(jnp.maximum(array, -reach), reach).astype(kind)


def setup_inputs(seed: int = 0, part: int = 0) -> dict:
    keys = jax.random.split(jax.random.key(seed), 9)
    own_keys = jax.random.split(jax.random.fold_in(keys[8], part), 9)
    potentials = scatter_about(own_keys[0], (ELECTRODE_COUNT, NZ, NXY), 1.0, 6.0, ((0, 2), (1, 8)))
    elec_order = jax.random.permutation(keys[1], ELECTRODE_COUNT).astype(jnp.int32)
    quadripoles = choose_distinct(keys[2], MEASURE_COUNT, ELECTRODE_COUNT, 4, 0)
    weighted_misfit = scatter_about(own_keys[3], (MEASURE_COUNT,), 1.0, 6.0)
    salinity = jnp.clip(jnp.exp(math.log(35.0) - 3.5553481 * jax.random.uniform(own_keys[4], (NZ, NXY), jnp.float32) ** block_levels(own_keys[4], (NZ, NXY), ((0, 8),), -0.2, 0.2)), 1.0, 35.0)
    water_content = jnp.clip(0.15 + 0.29999998 * jax.random.uniform(own_keys[5], (NZ, NXY), jnp.float32) ** block_levels(own_keys[5], (NZ, NXY), ((0, 8),), -0.2, 0.2), 0.15, 0.45)
    cementation = jnp.clip(jnp.exp(math.log(2.5) - 0.6539265 * jax.random.uniform(own_keys[6], (NZ, NXY), jnp.float32) ** block_levels(own_keys[6], (NZ, NXY), ((0, 8),), -0.2, 0.2)), 1.3, 2.5)
    anisotropy = jnp.clip(1.0 + 0.18 * jax.random.normal(own_keys[7], (3, NZ, NXY), jnp.float32), 0.1, 1.9)
    return {"potentials": potentials, "elec_order": elec_order, "quadripoles": quadripoles, "weighted_misfit": weighted_misfit, "salinity": salinity, "water_content": water_content, "cementation": cementation, "anisotropy": anisotropy}


def assemble_weights(quadripoles, weighted_misfit, elec_order):
    count = elec_order.shape[0]
    position = jnp.zeros((count,), jnp.int32).at[elec_order].set(jnp.arange(count, dtype=jnp.int32))
    ends = position[quadripoles]
    rows_all = jnp.concatenate([ends[:, 0], ends[:, 1], ends[:, 0], ends[:, 1]])
    cols_all = jnp.concatenate([ends[:, 2], ends[:, 3], ends[:, 3], ends[:, 2]])
    weights_f = weighted_misfit.astype(jnp.float32)
    values = jnp.concatenate([weights_f, weights_f, -weights_f, -weights_f])
    matrix = jnp.zeros((count, count), jnp.float32).at[rows_all, cols_all].add(values)
    return matrix.astype(jnp.bfloat16)


def field_gradients(extended):
    field = extended.astype(jnp.float32)
    rows_n = field.shape[0]
    layers = field.shape[1] - 2
    field = field.reshape(rows_n, layers + 2, NY, NX)
    along_z = 0.5 * (field[:, 2:] - field[:, :-2])
    middle = field[:, 1:-1]
    pad_y = jnp.pad(middle, ((0, 0), (0, 0), (1, 1), (0, 0)))
    along_y = 0.5 * (pad_y[:, :, 2:] - pad_y[:, :, :-2])
    pad_x = jnp.pad(middle, ((0, 0), (0, 0), (0, 0), (1, 1)))
    along_x = 0.5 * (pad_x[:, :, :, 2:] - pad_x[:, :, :, :-2])
    stacked = jnp.stack([along_z, along_y, along_x])
    return stacked.reshape(3, rows_n, layers * NY * NX).astype(jnp.bfloat16)


def reference(potentials, elec_order, quadripoles, weighted_misfit, salinity, water_content, cementation, anisotropy):
    weight_matrix = assemble_weights(quadripoles, weighted_misfit, elec_order)
    padded = jnp.pad(potentials, ((0, 0), (1, 1), (0, 0)))
    blocks = NZ // CZ

    def one_block(block):
        start = (block * CZ).astype(jnp.int32)
        extended = lax.dynamic_slice_in_dim(padded, start, CZ + 2, 1)
        gradients = field_gradients(extended)
        salt_b = lax.dynamic_slice_in_dim(salinity, start, CZ, 0).reshape(-1)
        water_b = lax.dynamic_slice_in_dim(water_content, start, CZ, 0).reshape(-1)
        cement_b = lax.dynamic_slice_in_dim(cementation, start, CZ, 0).reshape(-1)
        aniso_b = lax.dynamic_slice_in_dim(anisotropy, start, CZ, 1).reshape(3, -1)
        bulk = 0.15 * salt_b * water_b ** cement_b
        sensitivity = jnp.zeros_like(bulk)
        for component in range(3):
            mixed = jnp.dot(weight_matrix, gradients[component], preferred_element_type=jnp.float32)
            inner = jnp.sum(gradients[component].astype(jnp.float32) * mixed, axis=0)
            sensitivity = sensitivity + bulk * aniso_b[component] * inner
        return sensitivity / salt_b, cement_b * sensitivity / water_b

    salt_out, water_out = lax.map(one_block, jnp.arange(blocks, dtype=jnp.int32))
    return salt_out.reshape(NZ, NX * NY), water_out.reshape(NZ, NX * NY)
```

```python
import jax
import jax.numpy as jnp
from jax import lax
from jax.sharding import PartitionSpec as P

NX = 32
NY = 32


def assemble(quadripoles, weighted_misfit, order):
    left_side = (quadripoles[:, 0][None, :] == order[:, None]).astype(jnp.bfloat16) - (
        quadripoles[:, 1][None, :] == order[:, None]
    ).astype(jnp.bfloat16)
    third = quadripoles[:, 2][:, None] == order[None, :]
    fourth = quadripoles[:, 3][:, None] == order[None, :]
    signed = third.astype(jnp.float32) - fourth.astype(jnp.float32)
    right_side = (weighted_misfit.astype(jnp.float32)[:, None] * signed).astype(jnp.bfloat16)
    return jnp.dot(left_side, right_side, preferred_element_type=jnp.float32).astype(jnp.bfloat16)


def half_difference(upper, lower):
    return (0.5 * (upper.astype(jnp.float32) - lower.astype(jnp.float32))).astype(jnp.bfloat16)


def form(weights, grads):
    mixed = jnp.dot(weights, grads, preferred_element_type=jnp.float32)
    return jnp.sum(grads.astype(jnp.float32) * mixed, axis=0)


def local(potentials, elec_order, quadripoles, weighted_misfit, salinity, water_content, cementation, anisotropy):
    blocks = lax.axis_size("space")
    s = lax.axis_index("space")
    c = lax.axis_index("elec")
    rows, layers, cells = potentials.shape
    half = cells // 2
    odd = lax.rem(s, 2)
    to_mate = [(i, i ^ 1) for i in range(blocks)]
    back_two = [(i, (i - 2) % blocks if i % 2 == 0 else (i + 2) % blocks) for i in range(blocks)]
    swap = [(0, 1), (1, 0)]

    def cut(array, layer, start, width):
        return lax.dynamic_slice(array, (0, layer, start), (rows, 1, width)).reshape(rows, width)

    near = cut(potentials, odd, c * half, half)
    far = cut(potentials, 1 - odd, c * half, half)
    near_in_0 = lax.ppermute(near, "space", to_mate)
    far_in_0 = lax.ppermute(far, "space", back_two)

    halo = 128
    width = half + halo
    theirs = lax.dynamic_slice(potentials, (0, 0, (1 - c) * (half - halo)), (rows, layers, width))
    other = lax.ppermute(theirs, "elec", swap)
    own = lax.dynamic_slice(potentials, (0, 0, c * (half - halo)), (rows, layers, width))
    near_2 = cut(other, odd, c * halo, half)
    far_2 = cut(other, 1 - odd, c * halo, half)
    near_in_1 = lax.ppermute(near_2, "space", to_mate)
    far_in_1 = lax.ppermute(far_2, "space", back_two)

    order = jnp.roll(elec_order, -c * rows)
    weights = assemble(quadripoles, weighted_misfit, order)

    field = jnp.concatenate([own, other], axis=0).reshape(2 * rows, layers, width // NX, NX)
    pad_x = jnp.pad(lax.dynamic_slice_in_dim(field, c * (halo // NX), half // NX, 2), ((0, 0), (0, 0), (0, 0), (1, 1)))
    along_x = half_difference(pad_x[..., 2:], pad_x[..., :-2]).reshape(2 * rows, -1)
    pad_y = jnp.pad(field, ((0, 0), (0, 0), (1, 1), (0, 0)))
    pad_y = lax.dynamic_slice_in_dim(pad_y, c * (halo // NX), half // NX + 2, 2)
    along_y = half_difference(pad_y[:, :, 2:], pad_y[:, :, :-2]).reshape(2 * rows, -1)
    form_y = form(weights, along_y).reshape(layers, half)
    form_x = form(weights, along_x).reshape(layers, half)

    bulk = 0.15 * salinity * water_content**cementation
    mine = lax.dynamic_slice_in_dim(anisotropy, c * half, half, 2)
    flat = mine[1] * form_y + mine[2] * form_x
    flat_other = lax.ppermute(flat, "elec", swap)

    near_in = jnp.concatenate([near_in_0, near_in_1], axis=0)
    far_in = jnp.concatenate([far_in_0, far_in_1], axis=0)
    far_all = jnp.concatenate([far, far_2], axis=0)
    inside = jnp.where(odd == 1, s >= 2, s + 2 < blocks)
    grad_a = half_difference(far_all, near_in)
    grad_b = half_difference(far_in, jnp.where(inside, near_in, jnp.zeros_like(near_in)))
    form_a = form(weights, grad_a)
    form_b = form(weights, grad_b)

    def joint(pairs, cross):
        return [(2 * i + k, 2 * j + (k ^ cross)) for i, j in pairs for k in range(2)]

    ahead_two = [(j, i) for i, j in back_two]
    both = ("space", "elec")
    a_same = lax.ppermute(form_a, both, joint(to_mate, 0))
    a_cross = lax.ppermute(form_a, both, joint(to_mate, 1))
    b_same = lax.ppermute(form_b, both, joint(ahead_two, 0))
    b_cross = lax.ppermute(form_b, both, joint(ahead_two, 1))

    def whole(same, cross):
        return jnp.where(c == 0, jnp.concatenate([same, cross], -1), jnp.concatenate([cross, same], -1))

    from_mate = whole(a_same, a_cross)
    from_far = whole(b_same, b_cross)
    form_z = jnp.where(odd == 1, jnp.stack([from_mate, from_far]), jnp.stack([from_far, from_mate]))
    sensitivity = bulk * (anisotropy[0] * form_z + whole(flat, flat_other))
    return sensitivity / salinity, cementation * sensitivity / water_content


def solution(mesh):
    split = P(("slab", "space"), None)
    placed = (P("elec", ("slab", "space"), None), P(), P(), P("slab"), split, split, split, P(None, ("slab", "space"), None))
    return jax.shard_map(local, mesh=mesh, in_specs=placed, out_specs=(split, split), check_vma=False)
```

```python
import functools
import jax
import jax.numpy as jnp
from jax import lax
from jax.experimental import pallas as pl
from jax.experimental.pallas import tpu as pltpu
from jax.sharding import PartitionSpec as P

NX = 32
LANES = 128
VMEM = pl.BlockSpec(memory_space=pltpu.VMEM)
SMEM = pl.BlockSpec(memory_space=pltpu.SMEM)
MIB = 2**20


def call(kernel, outs, specs, name, scratch=(), limit=16, flops=0, moved=0):
    return pl.pallas_call(
        kernel,
        out_shape=outs,
        in_specs=specs,
        out_specs=jax.tree.map(lambda _: VMEM, outs),
        scratch_shapes=scratch,
        compiler_params=pltpu.CompilerParams(vmem_limit_bytes=limit * MIB),
        cost_estimate=pl.CostEstimate(flops=flops, bytes_accessed=moved, transcendentals=0),
        name=name,
    )


def dot(left, right):
    return jnp.dot(left, right, preferred_element_type=jnp.float32)


def own_kernel(place, field, near, far):
    odd, core = place[0], place[1]
    half = near.shape[1]
    step = 64
    for r in range(0, field.shape[0], step):
        rows = pl.ds(r, step)
        for k in range(2):

            @pl.when(core == k)
            def _():
                first = field[rows, 0, k * half : (k + 1) * half]
                second = field[rows, 1, k * half : (k + 1) * half]
                near[rows, :] = jnp.where(odd == 1, second, first)
                far[rows, :] = jnp.where(odd == 1, first, second)


def give_kernel(place, field, give, rim):
    odd, core = place[0], place[1]
    half = field.shape[2] // 2
    step = 64
    for r in range(0, field.shape[0], step):
        rows = pl.ds(r, step)
        for k in range(2):

            @pl.when(core == k)
            def _():
                first = field[rows, 0, :]
                second = field[rows, 1, :]
                near = jnp.where(odd == 1, second, first)
                far = jnp.where(odd == 1, first, second)
                other = slice((1 - k) * half, (2 - k) * half)
                mine = slice(half - LANES, half) if k == 0 else slice(half, half + LANES)
                theirs = slice(half, half + LANES) if k == 0 else slice(half - LANES, half)
                give[rows, :half] = near[:, other]
                give[rows, half : 2 * half] = far[:, other]
                give[rows, 2 * half : 2 * half + LANES] = near[:, mine]
                give[rows, 2 * half + LANES :] = far[:, mine]
                rim[rows, :LANES] = near[:, theirs]
                rim[rows, LANES:] = far[:, theirs]


def cross_kernel(weights, out):
    n = out.shape[0]
    out[...] = (weights[n:, :n].astype(jnp.float32) + weights[:n, n:].astype(jnp.float32).T).astype(out.dtype)


def x_change(block):
    x = lax.rem(lax.broadcasted_iota(jnp.int32, block.shape, 1), NX)
    back = pltpu.roll(block, 2, 1)
    return jnp.where(x == 0, 0.0, block) - jnp.where(x == 1, 0.0, back)


def y_change(blocks, rim, first):
    lane = lax.broadcasted_iota(jnp.int32, rim.shape, 1)
    turned = [pltpu.roll(block, 2 * NX, 1) for block in blocks]
    above = jnp.where(first, rim, 0.0)
    below = jnp.where(first, 0.0, pltpu.roll(rim, 2 * NX, 1))
    out = []
    for b, block in enumerate(blocks):
        if b == 0:
            upper = jnp.where(lane < NX, above, block)
            lower = jnp.where(lane < NX, turned[-1], jnp.where(lane < 2 * NX, below, turned[0]))
        else:
            upper = block
            lower = jnp.where(lane < 2 * NX, turned[b - 1], turned[b])
        out.append(upper - lower)
    return out


def plane_kernel(place, near, far, rim, other, weights, cross, out, delta):
    first = place[1] == 0
    rows, half = near.shape
    count = half // LANES
    step = 128
    for layer, own in enumerate((near, far)):
        for group in range(2):
            for r in range(0, rows, step):
                if group == 0:
                    body = own[r : r + step, :]
                    edge = rim[r : r + step, layer * LANES : (layer + 1) * LANES]
                else:
                    body = other[r : r + step, layer * half : (layer + 1) * half]
                    at = 2 * half + layer * LANES
                    edge = other[r : r + step, at : at + LANES]
                body, edge = body.astype(jnp.float32), edge.astype(jnp.float32)
                blocks = [body[:, b * LANES : (b + 1) * LANES] for b in range(count)]
                along_y = y_change(blocks, edge, first)
                along_x = [x_change(block) for block in blocks]
                at = group * rows + r
                delta[0, at : at + step, :] = jnp.concatenate(along_y, axis=1).astype(jnp.bfloat16)
                delta[1, at : at + step, :] = jnp.concatenate(along_x, axis=1).astype(jnp.bfloat16)
        for part in range(2):
            total = jnp.zeros((8, half), jnp.float32)
            for at in range(0, 2 * rows, 256):
                grads = delta[part, at : at + 256, :]
                if at < rows:
                    mixed = dot(weights[at : at + 256, :rows], delta[part, :rows, :])
                else:
                    mixed = dot(weights[at : at + 256, rows:], delta[part, rows:, :])
                    mixed = mixed + dot(cross[at - rows : at - rows + 256, :], delta[part, :rows, :])
                total = total + jnp.sum((grads.astype(jnp.float32) * mixed).reshape(-1, 8, half), axis=0)
            total = 0.25 * jnp.sum(total, axis=0, keepdims=True)
            if part == 0:
                total = pltpu.roll(jnp.broadcast_to(total, (8, half)), half - NX, 1)
            else:
                total = jnp.broadcast_to(total, (8, half))
                total = jnp.concatenate(
                    [pltpu.roll(total[:, b * LANES : (b + 1) * LANES], LANES - 1, 1) for b in range(count)], axis=1
                )
            out[2 * layer + part : 2 * layer + part + 1, :] = total[:1]


def differences(place, far, near_in, far_in, rows):
    inside = place[2] == 1
    near_v = near_in[rows, :].astype(jnp.float32)
    change_a = far[rows, :].astype(jnp.float32) - near_v
    change_b = far_in[rows, :].astype(jnp.float32) - jnp.where(inside, near_v, 0.0)
    return change_a.astype(jnp.bfloat16), change_b.astype(jnp.bfloat16)


def early_kernel(place, far, near_in, far_in, weights, cross, carry, out, delta):
    rows, half = far.shape
    for r in range(0, rows, 128):
        at = pl.ds(r, 128)
        delta[at, :half], delta[at, half:] = differences(place, far, near_in, far_in, at)
    total = jnp.zeros((8, 2 * half), jnp.float32)
    for r in range(0, rows, 256):
        mixed = dot(weights[r : r + 256, :rows], delta[...])
        carry[r : r + 256, :] = dot(cross[r : r + 256, :], delta[...])
        total = total + jnp.sum((delta[r : r + 256, :].astype(jnp.float32) * mixed).reshape(-1, 8, 2 * half), axis=0)
    out[...] = total


def late_kernel(place, far, near_in, far_in, weights, carry, early, out_a, out_b, delta):
    rows, half = far.shape
    for r in range(0, rows, 128):
        at = pl.ds(r, 128)
        delta[at, :half], delta[at, half:] = differences(place, far, near_in, far_in, at)
    total = early[...]
    for r in range(0, rows, 256):
        mixed = carry[r : r + 256, :] + dot(weights[rows + r : rows + r + 256, rows:], delta[...])
        total = total + jnp.sum((delta[r : r + 256, :].astype(jnp.float32) * mixed).reshape(-1, 8, 2 * half), axis=0)
    total = 0.25 * jnp.sum(total, axis=0, keepdims=True)
    out_a[...] = total[:, :half]
    out_b[...] = total[:, half:]


def assemble(quadripoles, weighted_misfit, order):
    left_side = (quadripoles[:, 0][None, :] == order[:, None]).astype(jnp.bfloat16) - (
        quadripoles[:, 1][None, :] == order[:, None]
    ).astype(jnp.bfloat16)
    third = quadripoles[:, 2][:, None] == order[None, :]
    fourth = quadripoles[:, 3][:, None] == order[None, :]
    signed = third.astype(jnp.float32) - fourth.astype(jnp.float32)
    right_side = (weighted_misfit.astype(jnp.float32)[:, None] * signed).astype(jnp.bfloat16)
    return dot(left_side, right_side).astype(jnp.bfloat16)


def local(potentials, elec_order, quadripoles, weighted_misfit, salinity, water_content, cementation, anisotropy):
    blocks = lax.axis_size("space")
    s = lax.axis_index("space")
    c = lax.axis_index("elec")
    rows, layers, cells = potentials.shape
    half = cells // 2
    odd = lax.rem(s, 2)
    to_mate = [(i, i ^ 1) for i in range(blocks)]
    back_two = [(i, (i - 2) % blocks if i % 2 == 0 else (i + 2) % blocks) for i in range(blocks)]
    swap = [(0, 1), (1, 0)]
    inside = jnp.where(odd == 1, s >= 2, s + 2 < blocks)
    place = jnp.stack([odd, c, inside.astype(jnp.int32)]).astype(jnp.int32)
    shape = jax.ShapeDtypeStruct
    bf16, f32 = jnp.bfloat16, jnp.float32

    near, far = call(
        own_kernel, (shape((rows, half), bf16), shape((rows, half), bf16)), [SMEM, VMEM], "own", moved=rows * cells * 4
    )(place, potentials)
    near_in_0 = lax.ppermute(near, "space", to_mate)
    far_in_0 = lax.ppermute(far, "space", back_two)

    give, rim = call(
        give_kernel,
        (shape((rows, 2 * half + 2 * LANES), bf16), shape((rows, 2 * LANES), bf16)),
        [SMEM, VMEM],
        "give",
        moved=rows * cells * 4,
    )(place, potentials)
    other = lax.ppermute(give, "elec", swap)
    near_2 = other[:, :half]
    far_2 = other[:, half : 2 * half]
    near_in_1 = lax.ppermute(near_2, "space", to_mate)
    far_in_1 = lax.ppermute(far_2, "space", back_two)

    order = jnp.where(c == 0, elec_order, jnp.concatenate([elec_order[rows:], elec_order[:rows]]))
    weights = assemble(quadripoles, weighted_misfit, order)
    cross = call(cross_kernel, shape((rows, rows), bf16), [VMEM], "cross", moved=4 * rows * rows * 2)(weights)

    big = 2 * rows * rows * half * 2
    forms = call(
        plane_kernel,
        shape((2 * layers, half), f32),
        [SMEM] + [VMEM] * 6,
        "plane",
        scratch=[pltpu.VMEM((2, 2 * rows, half), bf16)],
        flops=big * 6,
        moved=rows * cells * 16,
    )(place, near, far, rim, other, weights, cross)

    bulk = 0.15 * salinity * water_content**cementation
    forms = jnp.where(odd == 1, jnp.concatenate([forms[2:], forms[:2]]), forms)
    mine = jnp.where(c == 0, anisotropy[1:, :, :half], anisotropy[1:, :, half:])
    flat = mine[0] * forms[0::2] + mine[1] * forms[1::2]
    flat_other = lax.ppermute(flat, "elec", swap)

    carry, early = call(
        early_kernel,
        (shape((rows, 2 * half), f32), shape((8, 2 * half), f32)),
        [SMEM] + [VMEM] * 5,
        "early",
        scratch=[pltpu.VMEM((rows, 2 * half), bf16)],
        flops=big * 4,
        moved=rows * cells * 16,
    )(place, far, near_in_0, far_in_0, weights, cross)
    form_a, form_b = call(
        late_kernel,
        (shape((1, half), f32), shape((1, half), f32)),
        [SMEM] + [VMEM] * 6,
        "late",
        scratch=[pltpu.VMEM((rows, 2 * half), bf16)],
        flops=big * 2,
        moved=rows * cells * 16,
    )(place, far_2, near_in_1, far_in_1, weights, carry, early)

    def joint(pairs, cross):
        return [(2 * i + k, 2 * j + (k ^ cross)) for i, j in pairs for k in range(2)]

    ahead_two = [(j, i) for i, j in back_two]
    both = ("space", "elec")
    a_same = lax.ppermute(form_a, both, joint(to_mate, 0))
    a_cross = lax.ppermute(form_a, both, joint(to_mate, 1))
    b_same = lax.ppermute(form_b, both, joint(ahead_two, 0))
    b_cross = lax.ppermute(form_b, both, joint(ahead_two, 1))

    def whole(same, cross):
        return jnp.where(c == 0, jnp.concatenate([same, cross], -1), jnp.concatenate([cross, same], -1))

    from_mate = whole(a_same, a_cross)
    from_far = whole(b_same, b_cross)
    form_z = jnp.where(odd == 1, jnp.concatenate([from_mate, from_far]), jnp.concatenate([from_far, from_mate]))
    sensitivity = bulk * (anisotropy[0] * form_z + whole(flat, flat_other))
    return sensitivity / salinity, cementation * sensitivity / water_content


def solution(mesh):
    split = P(("slab", "space"), None)
    placed = (P("elec", ("slab", "space"), None), P(), P(), P("slab"), split, split, split, P(None, ("slab", "space"), None))
    return jax.shard_map(local, mesh=mesh, in_specs=placed, out_specs=(split, split), check_vma=False)
```

```python
import functools
import jax
import jax.numpy as jnp
from jax import lax
from jax.experimental import pallas as pl
from jax.experimental.pallas import tpu as pltpu
from jax.sharding import PartitionSpec as P

NX = 32
LANES = 128
VMEM = pl.BlockSpec(memory_space=pltpu.VMEM)
SMEM = pl.BlockSpec(memory_space=pltpu.SMEM)
MIB = 2**20
LATER = True
AFTER = True


def call(kernel, outs, specs, name, scratch=(), limit=8, flops=0, moved=0):
    return pl.pallas_call(
        kernel,
        out_shape=outs,
        in_specs=specs,
        out_specs=jax.tree.map(lambda _: VMEM, outs),
        scratch_shapes=scratch,
        compiler_params=pltpu.CompilerParams(vmem_limit_bytes=limit * MIB),
        cost_estimate=pl.CostEstimate(flops=flops, bytes_accessed=moved, transcendentals=0),
        name=name,
    )


def dot(left, right):
    return jnp.dot(left, right, preferred_element_type=jnp.float32)


def keep_kernel(place, field, near, far):
    odd, core = place[0], place[1]
    half = near.shape[1]
    for k in range(2):

        @pl.when(core == k)
        def _():
            near[...] = field[1 - odd, :, k * half : (k + 1) * half]
            far[...] = field[odd, :, k * half : (k + 1) * half]


def give_kernel(place, field, near, far, edge, rim):
    odd, core = place[0], place[1]
    half = near.shape[1]
    for k in range(2):
        low, high = slice(half - LANES, half), slice(half, half + LANES)
        inner, outer = (low, high) if k == 0 else (high, low)

        @pl.when(core == k)
        def _():
            near[...] = field[1 - odd, :, (1 - k) * half : (2 - k) * half]
            far[...] = field[odd, :, (1 - k) * half : (2 - k) * half]

            @pl.loop(0, field.shape[1], step=64)
            def _(r):
                rows = pl.ds(pl.multiple_of(r, 64), 64)
                edge[rows, :LANES] = field[1 - odd, rows, inner]
                edge[rows, LANES:] = field[odd, rows, inner]
                rim[rows, :LANES] = field[1 - odd, rows, outer]
                rim[rows, LANES:] = field[odd, rows, outer]


def cross_kernel(weights, out):
    n = out.shape[0]
    out[...] = (weights[n:, :n].astype(jnp.float32) + weights[:n, n:].astype(jnp.float32).T).astype(out.dtype)


def x_change(block):
    x = lax.rem(lax.broadcasted_iota(jnp.int32, block.shape, 1), NX)
    back = pltpu.roll(block, 2, 1)
    return jnp.where(x == 0, 0.0, block) - jnp.where(x == 1, 0.0, back)


def y_change(blocks, rim, first):
    lane = lax.broadcasted_iota(jnp.int32, rim.shape, 1)
    turned = [pltpu.roll(block, 2 * NX, 1) for block in blocks]
    above = jnp.where(first, rim, 0.0)
    below = jnp.where(first, 0.0, pltpu.roll(rim, 2 * NX, 1))
    out = []
    for b, block in enumerate(blocks):
        if b == 0:
            upper = jnp.where(lane < NX, above, block)
            lower = jnp.where(lane < NX, turned[-1], jnp.where(lane < 2 * NX, below, turned[0]))
        else:
            upper = block
            lower = jnp.where(lane < 2 * NX, turned[b - 1], turned[b])
        out.append(upper - lower)
    return out


def plane_kernel(place, near, far, rim, near_x, far_x, rim_x, weights, cross, out, delta):
    first = place[1] == 0
    rows, half = near.shape
    count = half // LANES
    step = 128
    for layer, own in enumerate(((near, near_x), (far, far_x))):
        for group in range(2):
            for r in range(0, rows, step):
                body = own[group][r : r + step, :]
                edge = (rim, rim_x)[group][r : r + step, layer * LANES : (layer + 1) * LANES]
                body, edge = body.astype(jnp.float32), edge.astype(jnp.float32)
                blocks = [body[:, b * LANES : (b + 1) * LANES] for b in range(count)]
                along_y = y_change(blocks, edge, first)
                along_x = [x_change(block) for block in blocks]
                at = group * rows + r
                delta[0, at : at + step, :] = jnp.concatenate(along_y, axis=1).astype(jnp.bfloat16)
                delta[1, at : at + step, :] = jnp.concatenate(along_x, axis=1).astype(jnp.bfloat16)
        for part in range(2):
            total = jnp.zeros((8, half), jnp.float32)
            for at in range(0, 2 * rows, 256):
                grads = delta[part, at : at + 256, :]
                if at < rows:
                    mixed = dot(weights[at : at + 256, :rows], delta[part, :rows, :])
                else:
                    mixed = dot(weights[at : at + 256, rows:], delta[part, rows:, :])
                    mixed = mixed + dot(cross[at - rows : at - rows + 256, :], delta[part, :rows, :])
                total = total + jnp.sum((grads.astype(jnp.float32) * mixed).reshape(-1, 8, half), axis=0)
            total = 0.25 * jnp.sum(total, axis=0, keepdims=True)
            if part == 0:
                total = pltpu.roll(jnp.broadcast_to(total, (8, half)), half - NX, 1)
            else:
                total = jnp.broadcast_to(total, (8, half))
                total = jnp.concatenate(
                    [pltpu.roll(total[:, b * LANES : (b + 1) * LANES], LANES - 1, 1) for b in range(count)], axis=1
                )
            out[2 * layer + part : 2 * layer + part + 1, :] = total[:1]


def differences(far, near_in, far_in, rows):
    near_v = near_in[rows, :].astype(jnp.float32)
    change_a = far[rows, :].astype(jnp.float32) - near_v
    change_b = far_in[rows, :].astype(jnp.float32) - near_v
    return change_a.astype(jnp.bfloat16), change_b.astype(jnp.bfloat16)


def early_kernel(far, near_in, far_in, weights, cross, carry, out, delta):
    rows, half = far.shape
    for r in range(0, rows, 128):
        at = pl.ds(r, 128)
        delta[at, :half], delta[at, half:] = differences(far, near_in, far_in, at)
    total = jnp.zeros((8, 2 * half), jnp.float32)
    for r in range(0, rows, 256):
        mixed = dot(weights[r : r + 256, :rows], delta[...])
        carry[r : r + 256, :] = dot(cross[r : r + 256, :], delta[...])
        total = total + jnp.sum((delta[r : r + 256, :].astype(jnp.float32) * mixed).reshape(-1, 8, 2 * half), axis=0)
    out[...] = total


def late_kernel(far, near_in, far_in, weights, carry, early, out_a, out_b, delta):
    rows, half = far.shape
    for r in range(0, rows, 128):
        at = pl.ds(r, 128)
        delta[at, :half], delta[at, half:] = differences(far, near_in, far_in, at)
    total = early[...]
    for r in range(0, rows, 256):
        mixed = carry[r : r + 256, :] + dot(weights[rows + r : rows + r + 256, rows:], delta[...])
        total = total + jnp.sum((delta[r : r + 256, :].astype(jnp.float32) * mixed).reshape(-1, 8, 2 * half), axis=0)
    total = 0.25 * jnp.sum(total, axis=0, keepdims=True)
    out_a[...] = total[:, :half]
    out_b[...] = total[:, half:]


def assemble(quadripoles, weighted_misfit, order):
    left_side = (quadripoles[:, 0][None, :] == order[:, None]).astype(jnp.bfloat16) - (
        quadripoles[:, 1][None, :] == order[:, None]
    ).astype(jnp.bfloat16)
    third = quadripoles[:, 2][:, None] == order[None, :]
    fourth = quadripoles[:, 3][:, None] == order[None, :]
    signed = third.astype(jnp.float32) - fourth.astype(jnp.float32)
    right_side = (weighted_misfit.astype(jnp.float32)[:, None] * signed).astype(jnp.bfloat16)
    return dot(left_side, right_side).astype(jnp.bfloat16)


def local(potentials, elec_order, quadripoles, weighted_misfit, salinity, water_content, cementation, anisotropy):
    blocks = lax.axis_size("space")
    s = lax.axis_index("space")
    c = lax.axis_index("elec")
    rows, layers, cells = potentials.shape
    half = cells // 2
    odd = lax.rem(s, 2)
    to_mate = [(i, i ^ 1) for i in range(blocks)]
    ahead = [(i, i - 2) for i in range(2, blocks, 2)] + [(i, i + 2) for i in range(1, blocks - 2, 2)]
    swap = [(0, 1), (1, 0)]
    place = jnp.stack([odd, c]).astype(jnp.int32)
    shape = jax.ShapeDtypeStruct
    bf16, f32 = jnp.bfloat16, jnp.float32
    both = ("space", "elec")

    def joint(pairs, cross):
        return [(2 * i + k, 2 * j + (k ^ cross)) for i, j in pairs for k in range(2)]

    field = jnp.transpose(potentials, (1, 0, 2))
    piece = shape((rows, half), bf16)
    strip = shape((rows, 2 * LANES), bf16)
    near, far = call(keep_kernel, (piece,) * 2, [SMEM, VMEM], "keep", moved=rows * cells * 4, limit=2)(place, field)
    near_in_0 = lax.ppermute(near, both, joint(to_mate, 0))
    far_in_0 = lax.ppermute(far, both, joint(ahead, 0))
    field, near, far = lax.optimization_barrier((field, near, far))
    near_give, far_give, edge, rim = call(
        give_kernel, (piece,) * 2 + (strip,) * 2, [SMEM, VMEM], "give", moved=rows * cells * 4, limit=2
    )(place, field)
    near_x = lax.ppermute(near_give, "elec", swap)
    far_x = lax.ppermute(far_give, "elec", swap)
    rim_x = lax.ppermute(edge, "elec", swap)

    order = jnp.where(c == 0, elec_order, jnp.concatenate([elec_order[rows:], elec_order[:rows]]))
    if AFTER:
        quadripoles, near_give = lax.optimization_barrier((quadripoles, near_give))
    weights = assemble(quadripoles, weighted_misfit, order)
    cross = call(cross_kernel, shape((rows, rows), bf16), [VMEM], "cross", moved=4 * rows * rows * 2)(weights)
    if LATER:
        near_give, far_give, weights = lax.optimization_barrier((near_give, far_give, weights))
    near_in_1 = lax.ppermute(near_give, both, joint(to_mate, 1))
    far_in_1 = lax.ppermute(far_give, both, joint(ahead, 1))

    big = 2 * rows * rows * half * 2
    forms = call(
        plane_kernel,
        shape((2 * layers, half), f32),
        [SMEM] + [VMEM] * 8,
        "plane",
        scratch=[pltpu.VMEM((2, 2 * rows, half), bf16)],
        limit=16,
        flops=big * 6,
        moved=rows * cells * 16,
    )(place, near, far, rim, near_x, far_x, rim_x, weights, cross)

    bulk = 0.15 * salinity * water_content**cementation
    salt_scale = bulk / salinity
    water_scale = bulk * cementation / water_content
    row = lax.broadcasted_iota(jnp.int32, (layers, cells), 0)
    is_near = row == 1 - odd
    is_mine = lax.broadcasted_iota(jnp.int32, (1, cells), 1) // half == c

    def spread(near_mine, near_other, far_mine, far_other):
        def line(mine, other):
            return jnp.where(is_mine, jnp.concatenate([mine, mine], 1), jnp.concatenate([other, other], 1))

        return jnp.where(is_near, line(near_mine, near_other), line(far_mine, far_other))

    forms_x = lax.ppermute(forms, "elec", swap)
    flat = anisotropy[1] * spread(forms[0:1], forms_x[0:1], forms[2:3], forms_x[2:3])
    flat = flat + anisotropy[2] * spread(forms[1:2], forms_x[1:2], forms[3:4], forms_x[3:4])
    salt_base, water_base = salt_scale * flat, water_scale * flat
    salt_scale, water_scale = salt_scale * anisotropy[0], water_scale * anisotropy[0]

    carry, early = call(
        early_kernel,
        (shape((rows, 2 * half), f32), shape((8, 2 * half), f32)),
        [VMEM] * 5,
        "early",
        scratch=[pltpu.VMEM((rows, 2 * half), bf16)],
        flops=big * 4,
        moved=rows * cells * 16,
    )(far, near_in_0, far_in_0, weights, cross)
    early, salt_base, water_base, salt_scale, water_scale = lax.optimization_barrier(
        (early, salt_base, water_base, salt_scale, water_scale)
    )
    form_a, form_b = call(
        late_kernel,
        (shape((1, half), f32), shape((1, half), f32)),
        [VMEM] * 6,
        "late",
        scratch=[pltpu.VMEM((rows, 2 * half), bf16)],
        flops=big * 2,
        moved=rows * cells * 16,
    )(far_x, near_in_1, far_in_1, weights, carry, early)

    b_cross = lax.ppermute(form_b, both, joint(to_mate, 1))
    b_same = lax.ppermute(form_b, both, joint(to_mate, 0))
    a_x = lax.ppermute(form_a, "elec", swap)
    form_z = spread(form_a, a_x, b_same, b_cross)
    return salt_scale * form_z + salt_base, water_scale * form_z + water_base


def solution(mesh):
    split = P(("slab", "space"), None)
    placed = (P("elec", ("slab", "space"), None), P(), P(), P("slab"), split, split, split, P(None, ("slab", "space"), None))
    return jax.shard_map(local, mesh=mesh, in_specs=placed, out_specs=(split, split), check_vma=False)
```

```python
import functools
import jax
import jax.numpy as jnp
from jax import lax
from jax.experimental import pallas as pl
from jax.experimental.pallas import tpu as pltpu
from jax.sharding import PartitionSpec as P

NX = 32
LANES = 128
VMEM = pl.BlockSpec(memory_space=pltpu.VMEM)
SMEM = pl.BlockSpec(memory_space=pltpu.SMEM)
MIB = 2**20
LATER = True
HOLD = True
AFTER = True


def call(kernel, outs, specs, name, scratch=(), limit=8, flops=0, moved=0):
    return pl.pallas_call(
        kernel,
        out_shape=outs,
        in_specs=specs,
        out_specs=jax.tree.map(lambda _: VMEM, outs),
        scratch_shapes=scratch,
        compiler_params=pltpu.CompilerParams(vmem_limit_bytes=limit * MIB),
        cost_estimate=pl.CostEstimate(flops=flops, bytes_accessed=moved, transcendentals=0),
        name=name,
    )


def dot(left, right):
    return jnp.dot(left, right, preferred_element_type=jnp.float32)


def keep_kernel(place, field, near, far):
    odd, core = place[0], place[1]
    half = near.shape[1]
    for k in range(2):

        @pl.when(core == k)
        def _():
            near[...] = field[1 - odd, :, k * half : (k + 1) * half]
            far[...] = field[odd, :, k * half : (k + 1) * half]


def give_kernel(place, field, near, far, parcel, rim):
    odd, core = place[0], place[1]
    half = near.shape[1]
    for k in range(2):
        low, high = slice(half - LANES, half), slice(half, half + LANES)
        inner, outer = (low, high) if k == 0 else (high, low)

        @pl.when(core == k)
        def _():
            near[...] = field[1 - odd, :, (1 - k) * half : (2 - k) * half]
            far[...] = field[odd, :, (1 - k) * half : (2 - k) * half]
            parcel[:, :half] = field[1 - odd, :, (1 - k) * half : (2 - k) * half]
            parcel[:, half : 2 * half] = field[odd, :, (1 - k) * half : (2 - k) * half]
            parcel[:, 2 * half : 2 * half + LANES] = field[1 - odd, :, inner]
            parcel[:, 2 * half + LANES :] = field[odd, :, inner]
            rim[:, :LANES] = field[1 - odd, :, outer]
            rim[:, LANES:] = field[odd, :, outer]


def cross_kernel(weights, out):
    n = out.shape[0]
    out[...] = (weights[n:, :n].astype(jnp.float32) + weights[:n, n:].astype(jnp.float32).T).astype(out.dtype)


def x_change(block):
    x = lax.rem(lax.broadcasted_iota(jnp.int32, block.shape, 1), NX)
    back = pltpu.roll(block, 2, 1)
    return jnp.where(x == 0, 0.0, block) - jnp.where(x == 1, 0.0, back)


def y_change(blocks, rim, first):
    lane = lax.broadcasted_iota(jnp.int32, rim.shape, 1)
    turned = [pltpu.roll(block, 2 * NX, 1) for block in blocks]
    above = jnp.where(first, rim, 0.0)
    below = jnp.where(first, 0.0, pltpu.roll(rim, 2 * NX, 1))
    out = []
    for b, block in enumerate(blocks):
        if b == 0:
            upper = jnp.where(lane < NX, above, block)
            lower = jnp.where(lane < NX, turned[-1], jnp.where(lane < 2 * NX, below, turned[0]))
        else:
            upper = block
            lower = jnp.where(lane < 2 * NX, turned[b - 1], turned[b])
        out.append(upper - lower)
    return out


def plane_kernel(place, near, far, rim, parcel, weights, cross, out, delta):
    first = place[1] == 0
    rows, half = near.shape
    count = half // LANES
    step = 128
    for layer, own in enumerate((near, far)):
        for group in range(2):
            for r in range(0, rows, step):
                at = pl.ds(r, step)
                if group == 0:
                    body = own[at, :]
                    edge = rim[at, layer * LANES : (layer + 1) * LANES]
                else:
                    body = parcel[at, layer * half : (layer + 1) * half]
                    edge = parcel[at, 2 * half + layer * LANES : 2 * half + (layer + 1) * LANES]
                body, edge = body.astype(jnp.float32), edge.astype(jnp.float32)
                blocks = [body[:, b * LANES : (b + 1) * LANES] for b in range(count)]
                along_y = y_change(blocks, edge, first)
                along_x = [x_change(block) for block in blocks]
                at = group * rows + r
                delta[0, at : at + step, :] = jnp.concatenate(along_y, axis=1).astype(jnp.bfloat16)
                delta[1, at : at + step, :] = jnp.concatenate(along_x, axis=1).astype(jnp.bfloat16)
        for part in range(2):
            total = jnp.zeros((8, half), jnp.float32)
            for at in range(0, 2 * rows, 256):
                grads = delta[part, at : at + 256, :]
                if at < rows:
                    mixed = dot(weights[at : at + 256, :rows], delta[part, :rows, :])
                else:
                    mixed = dot(weights[at : at + 256, rows:], delta[part, rows:, :])
                    mixed = mixed + dot(cross[at - rows : at - rows + 256, :], delta[part, :rows, :])
                total = total + jnp.sum((grads.astype(jnp.float32) * mixed).reshape(-1, 8, half), axis=0)
            total = 0.25 * jnp.sum(total, axis=0, keepdims=True)
            if part == 0:
                total = pltpu.roll(jnp.broadcast_to(total, (8, half)), half - NX, 1)
            else:
                total = jnp.broadcast_to(total, (8, half))
                total = jnp.concatenate(
                    [pltpu.roll(total[:, b * LANES : (b + 1) * LANES], LANES - 1, 1) for b in range(count)], axis=1
                )
            out[2 * layer + part : 2 * layer + part + 1, :] = total[:1]


def differences(far, near_in, far_in, rows):
    near_v = near_in[rows, :].astype(jnp.float32)
    change_a = far[rows, :].astype(jnp.float32) - near_v
    change_b = far_in[rows, :].astype(jnp.float32) - near_v
    return change_a.astype(jnp.bfloat16), change_b.astype(jnp.bfloat16)


def early_kernel(far, near_in, far_in, weights, cross, carry_a, carry_b, out_a, out_b, delta):
    rows, half = far.shape
    for r in range(0, rows, 128):
        at = pl.ds(r, 128)
        delta[at, :half], delta[at, half:] = differences(far, near_in, far_in, at)
    total = jnp.zeros((8, 2 * half), jnp.float32)
    for r in range(0, rows, 256):
        mixed = dot(weights[r : r + 256, :rows], delta[...])
        carry = dot(cross[r : r + 256, :], delta[...])
        carry_a[r : r + 256, :] = carry[:, :half]
        carry_b[r : r + 256, :] = carry[:, half:]
        total = total + jnp.sum((delta[r : r + 256, :].astype(jnp.float32) * mixed).reshape(-1, 8, 2 * half), axis=0)
    out_a[...] = total[:, :half]
    out_b[...] = total[:, half:]


def close_kernel(upper, lower, weights, carry, early, out, start=0):
    rows, half = lower.shape
    upper = upper.at[:, start : start + half]
    changes = [(upper[r : r + 128, :].astype(jnp.float32) - lower[r : r + 128, :].astype(jnp.float32)) for r in range(0, rows, 128)]
    delta = jnp.concatenate(changes, axis=0).astype(jnp.bfloat16)
    total = early[...]
    for r in range(0, rows, 256):
        mixed = carry[r : r + 256, :] + dot(weights[rows + r : rows + r + 256, rows:], delta)
        total = total + jnp.sum((delta[r : r + 256, :].astype(jnp.float32) * mixed).reshape(-1, 8, half), axis=0)
    out[...] = 0.25 * jnp.sum(total, axis=0, keepdims=True)


def assemble(quadripoles, weighted_misfit, order):
    left_side = (quadripoles[:, 0][None, :] == order[:, None]).astype(jnp.bfloat16) - (
        quadripoles[:, 1][None, :] == order[:, None]
    ).astype(jnp.bfloat16)
    third = quadripoles[:, 2][:, None] == order[None, :]
    fourth = quadripoles[:, 3][:, None] == order[None, :]
    signed = third.astype(jnp.float32) - fourth.astype(jnp.float32)
    right_side = (weighted_misfit.astype(jnp.float32)[:, None] * signed).astype(jnp.bfloat16)
    return dot(left_side, right_side).astype(jnp.bfloat16)


def local(potentials, elec_order, quadripoles, weighted_misfit, salinity, water_content, cementation, anisotropy):
    blocks = lax.axis_size("space")
    s = lax.axis_index("space")
    c = lax.axis_index("elec")
    rows, layers, cells = potentials.shape
    half = cells // 2
    odd = lax.rem(s, 2)
    to_mate = [(i, i ^ 1) for i in range(blocks)]
    ahead = [(i, i - 2) for i in range(2, blocks, 2)] + [(i, i + 2) for i in range(1, blocks - 2, 2)]
    swap = [(0, 1), (1, 0)]
    low_core, near_level = c == 0, 1 - odd
    potentials, odd, c, low_core, near_level = lax.optimization_barrier((potentials, odd, c, low_core, near_level))
    place = jnp.stack([odd, c]).astype(jnp.int32)
    shape = jax.ShapeDtypeStruct
    bf16, f32 = jnp.bfloat16, jnp.float32
    both = ("space", "elec")

    def joint(pairs, cross):
        return [(2 * i + k, 2 * j + (k ^ cross)) for i, j in pairs for k in range(2)]

    field = jnp.transpose(potentials, (1, 0, 2))
    piece = shape((rows, half), bf16)
    strip = shape((rows, 2 * LANES), bf16)
    near, far = call(keep_kernel, (piece,) * 2, [SMEM, VMEM], "keep", moved=rows * cells * 4, limit=2)(place, field)
    near_in_0 = lax.ppermute(near, both, joint(to_mate, 0))
    far_in_0 = lax.ppermute(far, both, joint(ahead, 0))
    field, near, far = lax.optimization_barrier((field, near, far))
    near_give, far_give, parcel, rim = call(
        give_kernel,
        (piece, piece, shape((rows, 2 * half + 2 * LANES), bf16), strip),
        [SMEM, VMEM],
        "give",
        moved=rows * cells * 8,
        limit=2,
    )(place, field)
    parcel = lax.ppermute(parcel, "elec", swap)

    order = jnp.where(low_core, elec_order, jnp.concatenate([elec_order[rows:], elec_order[:rows]]))
    if AFTER:
        quadripoles, near_give = lax.optimization_barrier((quadripoles, near_give))
    weights = assemble(quadripoles, weighted_misfit, order)
    cross = call(cross_kernel, shape((rows, rows), bf16), [VMEM], "cross", moved=4 * rows * rows * 2)(weights)
    near_give, weights = lax.optimization_barrier((near_give, weights))
    far_give, cross = lax.optimization_barrier((far_give, cross))
    near_in_1 = lax.ppermute(near_give, both, joint(to_mate, 1))
    far_in_1 = lax.ppermute(far_give, both, joint(ahead, 1))

    big = 2 * rows * rows * half * 2
    forms = call(
        plane_kernel,
        shape((2 * layers, half), f32),
        [SMEM] + [VMEM] * 6,
        "plane",
        scratch=[pltpu.VMEM((2, 2 * rows, half), bf16)],
        limit=16,
        flops=big * 6,
        moved=rows * cells * 16,
    )(place, near, far, rim, parcel, weights, cross)

    bulk = 0.15 * salinity * water_content**cementation
    salt_scale = bulk / salinity
    water_scale = bulk * cementation / water_content
    row = lax.broadcasted_iota(jnp.int32, (layers, cells), 0)
    is_near = row == near_level
    is_mine = lax.broadcasted_iota(jnp.int32, (1, cells), 1) // half == c

    def spread(near_mine, near_other, far_mine, far_other):
        def line(mine, other):
            return jnp.where(is_mine, jnp.concatenate([mine, mine], 1), jnp.concatenate([other, other], 1))

        return jnp.where(is_near, line(near_mine, near_other), line(far_mine, far_other))

    forms_x = lax.ppermute(forms, "elec", swap)
    flat = anisotropy[1] * spread(forms[0:1], forms_x[0:1], forms[2:3], forms_x[2:3])
    flat = flat + anisotropy[2] * spread(forms[1:2], forms_x[1:2], forms[3:4], forms_x[3:4])
    salt_base, water_base = salt_scale * flat, water_scale * flat
    salt_scale, water_scale = salt_scale * anisotropy[0], water_scale * anisotropy[0]

    weights_e, forms = lax.optimization_barrier((weights, forms))
    carry_a, carry_b, early_a, early_b = call(
        early_kernel,
        (shape((rows, half), f32),) * 2 + (shape((8, half), f32),) * 2,
        [VMEM] * 5,
        "early",
        scratch=[pltpu.VMEM((rows, 2 * half), bf16)],
        flops=big * 4,
        moved=rows * cells * 16,
    )(far, near_in_0, far_in_0, weights_e, cross)
    early_a, salt_base, water_base, salt_scale, water_scale = lax.optimization_barrier(
        (early_a, salt_base, water_base, salt_scale, water_scale)
    )

    def close(name, start, *given):
        return call(
            functools.partial(close_kernel, start=start), shape((1, half), f32), [VMEM] * 5, name, flops=big, moved=rows * cells * 8, limit=6
        )(*given)

    form_a = close("close_a", half, parcel, near_in_1, weights, carry_a, early_a)
    a_x = lax.ppermute(form_a, "elec", swap)
    if HOLD:
        far_in_1, form_a = lax.optimization_barrier((far_in_1, form_a))
    form_b = close("close_b", 0, far_in_1, near_in_1, weights, carry_b, early_b)
    b_cross = lax.ppermute(form_b, both, joint(to_mate, 1))
    b_same = lax.ppermute(form_b, both, joint(to_mate, 0))
    form_z = spread(form_a, a_x, b_same, b_cross)
    return salt_scale * form_z + salt_base, water_scale * form_z + water_base


def solution(mesh):
    split = P(("slab", "space"), None)
    placed = (P("elec", ("slab", "space"), None), P(), P(), P("slab"), split, split, split, P(None, ("slab", "space"), None))
    return jax.shard_map(local, mesh=mesh, in_specs=placed, out_specs=(split, split), check_vma=False)
```

```python
import functools
import jax
import jax.numpy as jnp
from jax import lax
from jax.experimental import pallas as pl
from jax.experimental.pallas import tpu as pltpu
from jax.sharding import PartitionSpec as P

NX = 32
LANES = 128
VMEM = pl.BlockSpec(memory_space=pltpu.VMEM)
SMEM = pl.BlockSpec(memory_space=pltpu.SMEM)
MIB = 2**20
FIRST = 51
HOLD = True


def call(kernel, outs, specs, name, scratch=(), limit=8, flops=0, moved=0):
    return pl.pallas_call(
        kernel,
        out_shape=outs,
        in_specs=specs,
        out_specs=jax.tree.map(lambda _: VMEM, outs),
        scratch_shapes=scratch,
        compiler_params=pltpu.CompilerParams(vmem_limit_bytes=limit * MIB),
        cost_estimate=pl.CostEstimate(flops=flops, bytes_accessed=moved, transcendentals=0),
        name=name,
    )


def dot(left, right):
    return jnp.dot(left, right, preferred_element_type=jnp.float32)


def levels(block, odd):
    layers = jnp.swapaxes(block, 0, 1)
    return jnp.where(odd == 1, layers[0], layers[1]), jnp.where(odd == 1, layers[1], layers[0])


def keep_kernel(place, potentials, near, far, raw, sems):
    odd, core = place[0], place[1]
    rows, half = near.shape
    size = rows // sems.shape[0]
    cells = pl.ds(pl.multiple_of(core * half, LANES), half)
    copies = []
    for i in range(sems.shape[0]):
        part = pl.ds(i * size, size)
        copies.append(pltpu.make_async_copy(potentials.at[part, :, cells], raw.at[part], sems.at[i]))
        copies[-1].start()
    for i, copy in enumerate(copies):
        copy.wait()
        for r in range(i * size, (i + 1) * size, 32):
            near[r : r + 32, :], far[r : r + 32, :] = levels(raw[r : r + 32], odd)


def give_kernel(place, potentials, near, far, parcel, rim):
    odd, core = place[0], place[1]
    rows, half = near.shape
    for k in range(2):
        low, high = slice(half - LANES, half), slice(half, half + LANES)
        inner, outer = (low, high) if k == 0 else (high, low)
        theirs = slice((1 - k) * half, (2 - k) * half)

        @pl.when(core == k)
        def _():
            for r in range(0, rows, 32):
                at = slice(r, r + 32)
                near_v, far_v = levels(potentials[at], odd)
                near[at, :] = near_v[:, theirs]
                far[at, :] = far_v[:, theirs]
                parcel[at, :half] = near_v[:, theirs]
                parcel[at, half : 2 * half] = far_v[:, theirs]
                parcel[at, 2 * half : 2 * half + LANES] = near_v[:, inner]
                parcel[at, 2 * half + LANES :] = far_v[:, inner]
                rim[at, :LANES] = near_v[:, outer]
                rim[at, LANES:] = far_v[:, outer]


def cross_kernel(weights, out):
    n = out.shape[0]
    out[...] = (weights[n:, :n].astype(jnp.float32) + weights[:n, n:].astype(jnp.float32).T).astype(out.dtype)


def x_change(block):
    x = lax.rem(lax.broadcasted_iota(jnp.int32, block.shape, 1), NX)
    back = pltpu.roll(block, 2, 1)
    return jnp.where(x == 0, 0.0, block) - jnp.where(x == 1, 0.0, back)


def y_change(blocks, rim, first):
    lane = lax.broadcasted_iota(jnp.int32, rim.shape, 1)
    turned = [pltpu.roll(block, 2 * NX, 1) for block in blocks]
    above = jnp.where(first, rim, 0.0)
    below = jnp.where(first, 0.0, pltpu.roll(rim, 2 * NX, 1))
    out = []
    for b, block in enumerate(blocks):
        if b == 0:
            upper = jnp.where(lane < NX, above, block)
            lower = jnp.where(lane < NX, turned[-1], jnp.where(lane < 2 * NX, below, turned[0]))
        else:
            upper = block
            lower = jnp.where(lane < 2 * NX, turned[b - 1], turned[b])
        out.append(upper - lower)
    return out


def plane_kernel(place, near, far, rim, parcel, weights, cross, out, delta):
    first = place[1] == 0
    rows, half = near.shape
    count = half // LANES
    step = 128
    for layer, own in enumerate((near, far)):
        for group in range(2):
            for r in range(0, rows, step):
                at = pl.ds(r, step)
                if group == 0:
                    body = own[at, :]
                    edge = rim[at, layer * LANES : (layer + 1) * LANES]
                else:
                    body = parcel[at, layer * half : (layer + 1) * half]
                    edge = parcel[at, 2 * half + layer * LANES : 2 * half + (layer + 1) * LANES]
                body, edge = body.astype(jnp.float32), edge.astype(jnp.float32)
                blocks = [body[:, b * LANES : (b + 1) * LANES] for b in range(count)]
                along_y = y_change(blocks, edge, first)
                along_x = [x_change(block) for block in blocks]
                at = group * rows + r
                delta[0, at : at + step, :] = jnp.concatenate(along_y, axis=1).astype(jnp.bfloat16)
                delta[1, at : at + step, :] = jnp.concatenate(along_x, axis=1).astype(jnp.bfloat16)
        for part in range(2):
            total = jnp.zeros((8, half), jnp.float32)
            for at in range(0, 2 * rows, 256):
                grads = delta[part, at : at + 256, :]
                if at < rows:
                    mixed = dot(weights[at : at + 256, :rows], delta[part, :rows, :])
                else:
                    mixed = dot(weights[at : at + 256, rows:], delta[part, rows:, :])
                    mixed = mixed + dot(cross[at - rows : at - rows + 256, :], delta[part, :rows, :])
                total = total + jnp.sum((grads.astype(jnp.float32) * mixed).reshape(-1, 8, half), axis=0)
            total = 0.25 * jnp.sum(total, axis=0, keepdims=True)
            if part == 0:
                total = pltpu.roll(jnp.broadcast_to(total, (8, half)), half - NX, 1)
            else:
                total = jnp.broadcast_to(total, (8, half))
                total = jnp.concatenate(
                    [pltpu.roll(total[:, b * LANES : (b + 1) * LANES], LANES - 1, 1) for b in range(count)], axis=1
                )
            out[2 * layer + part : 2 * layer + part + 1, :] = total[:1]


def differences(far, near_in, far_in, rows):
    near_v = near_in[rows, :].astype(jnp.float32)
    change_a = far[rows, :].astype(jnp.float32) - near_v
    change_b = far_in[rows, :].astype(jnp.float32) - near_v
    return change_a.astype(jnp.bfloat16), change_b.astype(jnp.bfloat16)


def early_kernel(far, near_in, far_in, weights, cross, carry_a, carry_b, out_a, out_b, delta):
    rows, half = far.shape
    for r in range(0, rows, 128):
        at = pl.ds(r, 128)
        delta[at, :half], delta[at, half:] = differences(far, near_in, far_in, at)
    total = jnp.zeros((8, 2 * half), jnp.float32)
    for r in range(0, rows, 256):
        mixed = dot(weights[r : r + 256, :rows], delta[...])
        carry = dot(cross[r : r + 256, :], delta[...])
        carry_a[r : r + 256, :] = carry[:, :half]
        carry_b[r : r + 256, :] = carry[:, half:]
        total = total + jnp.sum((delta[r : r + 256, :].astype(jnp.float32) * mixed).reshape(-1, 8, 2 * half), axis=0)
    out_a[...] = total[:, :half]
    out_b[...] = total[:, half:]


def close_kernel(upper, lower, weights, carry, early, out, start=0):
    rows, half = lower.shape
    upper = upper.at[:, start : start + half]
    changes = [(upper[r : r + 128, :].astype(jnp.float32) - lower[r : r + 128, :].astype(jnp.float32)) for r in range(0, rows, 128)]
    delta = jnp.concatenate(changes, axis=0).astype(jnp.bfloat16)
    total = early[...]
    for r in range(0, rows, 256):
        mixed = carry[r : r + 256, :] + dot(weights[rows + r : rows + r + 256, rows:], delta)
        total = total + jnp.sum((delta[r : r + 256, :].astype(jnp.float32) * mixed).reshape(-1, 8, half), axis=0)
    out[...] = 0.25 * jnp.sum(total, axis=0, keepdims=True)


def assemble(quadripoles, weighted_misfit, order):
    left_side = (quadripoles[:, 0][None, :] == order[:, None]).astype(jnp.bfloat16) - (
        quadripoles[:, 1][None, :] == order[:, None]
    ).astype(jnp.bfloat16)
    third = quadripoles[:, 2][:, None] == order[None, :]
    fourth = quadripoles[:, 3][:, None] == order[None, :]
    signed = third.astype(jnp.float32) - fourth.astype(jnp.float32)
    right_side = (weighted_misfit.astype(jnp.float32)[:, None] * signed).astype(jnp.bfloat16)
    return dot(left_side, right_side).astype(jnp.bfloat16)


def local(potentials, elec_order, quadripoles, weighted_misfit, salinity, water_content, cementation, anisotropy):
    blocks = lax.axis_size("space")
    s = lax.axis_index("space")
    c = lax.axis_index("elec")
    rows, layers, cells = potentials.shape
    half = cells // 2
    odd = lax.rem(s, 2)
    to_mate = [(i, i ^ 1) for i in range(blocks)]
    ahead = [(i, i - 2) for i in range(2, blocks, 2)] + [(i, i + 2) for i in range(1, blocks - 2, 2)]
    swap = [(0, 1), (1, 0)]
    low_core, near_level = c == 0, 1 - odd
    potentials, odd, c, low_core, near_level = lax.optimization_barrier((potentials, odd, c, low_core, near_level))
    place = jnp.stack([odd, c]).astype(jnp.int32)
    shape = jax.ShapeDtypeStruct
    bf16, f32 = jnp.bfloat16, jnp.float32
    both = ("space", "elec")

    def joint(pairs, cross):
        return [(2 * i + k, 2 * j + (k ^ cross)) for i, j in pairs for k in range(2)]

    piece = shape((rows, half), bf16)
    strip = shape((rows, 2 * LANES), bf16)
    near, far = call(
        keep_kernel,
        (piece,) * 2,
        [SMEM, pl.BlockSpec(memory_space=pl.ANY)],
        "keep",
        scratch=[pltpu.VMEM((rows, layers, half), bf16), pltpu.SemaphoreType.DMA((4,))],
        moved=rows * cells * 4,
        limit=FIRST,
    )(place, potentials)
    near_in_0 = lax.ppermute(near, both, joint(to_mate, 0))
    far_in_0 = lax.ppermute(far, both, joint(ahead, 0))
    place_b, near, far, potentials = lax.optimization_barrier((place, near, far, potentials))
    near_give, far_give, parcel, rim = call(
        give_kernel,
        (piece, piece, shape((rows, 2 * half + 2 * LANES), bf16), strip),
        [SMEM, VMEM],
        "give",
        moved=rows * cells * 8,
        limit=4,
    )(place_b, potentials)
    parcel = lax.ppermute(parcel, "elec", swap)

    order = jnp.where(low_core, elec_order, jnp.concatenate([elec_order[rows:], elec_order[:rows]]))
    if True:
        quadripoles, near_give = lax.optimization_barrier((quadripoles, near_give))
    weights = assemble(quadripoles, weighted_misfit, order)
    cross = call(cross_kernel, shape((rows, rows), bf16), [VMEM], "cross", moved=4 * rows * rows * 2)(weights)
    near_give, weights = lax.optimization_barrier((near_give, weights))
    far_give, cross = lax.optimization_barrier((far_give, cross))
    near_in_1 = lax.ppermute(near_give, both, joint(to_mate, 1))
    far_in_1 = lax.ppermute(far_give, both, joint(ahead, 1))

    big = 2 * rows * rows * half * 2
    forms = call(
        plane_kernel,
        shape((2 * layers, half), f32),
        [SMEM] + [VMEM] * 6,
        "plane",
        scratch=[pltpu.VMEM((2, 2 * rows, half), bf16)],
        limit=16,
        flops=big * 6,
        moved=rows * cells * 16,
    )(place, near, far, rim, parcel, weights, cross)

    bulk = 0.15 * salinity * water_content**cementation
    salt_scale = bulk / salinity
    water_scale = bulk * cementation / water_content
    row = lax.broadcasted_iota(jnp.int32, (layers, cells), 0)
    is_near = row == near_level
    is_mine = lax.broadcasted_iota(jnp.int32, (1, cells), 1) // half == c

    def spread(near_mine, near_other, far_mine, far_other):
        def line(mine, other):
            return jnp.where(is_mine, jnp.concatenate([mine, mine], 1), jnp.concatenate([other, other], 1))

        return jnp.where(is_near, line(near_mine, near_other), line(far_mine, far_other))

    forms_x = lax.ppermute(forms, "elec", swap)
    flat = anisotropy[1] * spread(forms[0:1], forms_x[0:1], forms[2:3], forms_x[2:3])
    flat = flat + anisotropy[2] * spread(forms[1:2], forms_x[1:2], forms[3:4], forms_x[3:4])
    salt_base, water_base = salt_scale * flat, water_scale * flat
    salt_scale, water_scale = salt_scale * anisotropy[0], water_scale * anisotropy[0]

    weights_e, forms = lax.optimization_barrier((weights, forms))
    carry_a, carry_b, early_a, early_b = call(
        early_kernel,
        (shape((rows, half), f32),) * 2 + (shape((8, half), f32),) * 2,
        [VMEM] * 5,
        "early",
        scratch=[pltpu.VMEM((rows, 2 * half), bf16)],
        flops=big * 4,
        moved=rows * cells * 16,
    )(far, near_in_0, far_in_0, weights_e, cross)
    early_a, salt_base, water_base, salt_scale, water_scale = lax.optimization_barrier(
        (early_a, salt_base, water_base, salt_scale, water_scale)
    )

    def close(name, start, *given):
        return call(
            functools.partial(close_kernel, start=start), shape((1, half), f32), [VMEM] * 5, name, flops=big, moved=rows * cells * 8, limit=6
        )(*given)

    form_a = close("close_a", half, parcel, near_in_1, weights, carry_a, early_a)
    a_x = lax.ppermute(form_a, "elec", swap)
    if HOLD:
        far_in_1, form_a = lax.optimization_barrier((far_in_1, form_a))
    form_b = close("close_b", 0, far_in_1, near_in_1, weights, carry_b, early_b)
    b_cross = lax.ppermute(form_b, both, joint(to_mate, 1))
    b_same = lax.ppermute(form_b, both, joint(to_mate, 0))
    form_z = spread(form_a, a_x, b_same, b_cross)
    return salt_scale * form_z + salt_base, water_scale * form_z + water_base


def solution(mesh):
    split = P(("slab", "space"), None)
    placed = (P("elec", ("slab", "space"), None), P(), P(), P("slab"), split, split, split, P(None, ("slab", "space"), None))
    return jax.shard_map(local, mesh=mesh, in_specs=placed, out_specs=(split, split), check_vma=False)
```

```python
import functools
import jax
import jax.numpy as jnp
from jax import lax
from jax.experimental import pallas as pl
from jax.experimental.pallas import tpu as pltpu
from jax.sharding import PartitionSpec as P

NX = 32
LANES = 128
VMEM = pl.BlockSpec(memory_space=pltpu.VMEM)
MIB = 2**20
FIRST = 51
HOLD = True


def call(kernel, outs, specs, name, scratch=(), limit=8, flops=0, moved=0):
    return pl.pallas_call(
        kernel,
        out_shape=outs,
        in_specs=specs,
        out_specs=jax.tree.map(lambda _: VMEM, outs),
        scratch_shapes=scratch,
        compiler_params=pltpu.CompilerParams(vmem_limit_bytes=limit * MIB),
        cost_estimate=pl.CostEstimate(flops=flops, bytes_accessed=moved, transcendentals=0),
        name=name,
    )


def dot(left, right):
    return jnp.dot(left, right, preferred_element_type=jnp.float32)


def spot():
    index = lax.axis_index("space")
    odd = lax.rem(index, 2)
    inside = jnp.where(odd == 1, index >= 2, index + 2 < lax.axis_size("space"))
    return odd, lax.axis_index("elec"), inside


def levels(block, odd):
    layers = jnp.swapaxes(block, 0, 1)
    return jnp.where(odd == 1, layers[0], layers[1]), jnp.where(odd == 1, layers[1], layers[0])


def keep_kernel(potentials, near, far, raw, sems):
    odd, core, _ = spot()
    rows, half = near.shape
    size = rows // sems.shape[0]
    cells = pl.ds(pl.multiple_of(core * half, LANES), half)
    copies = []
    for i in range(sems.shape[0]):
        part = pl.ds(i * size, size)
        copies.append(pltpu.make_async_copy(potentials.at[part, :, cells], raw.at[part], sems.at[i]))
        copies[-1].start()
    for i, copy in enumerate(copies):
        copy.wait()
        for r in range(i * size, (i + 1) * size, 32):
            near[r : r + 32, :], far[r : r + 32, :] = levels(raw[r : r + 32], odd)


def give_kernel(potentials, near, far, parcel, rim):
    odd, core, _ = spot()
    rows, half = near.shape
    for k in range(2):
        low, high = slice(half - LANES, half), slice(half, half + LANES)
        inner, outer = (low, high) if k == 0 else (high, low)
        theirs = slice((1 - k) * half, (2 - k) * half)

        @pl.when(core == k)
        def _():
            for r in range(0, rows, 32):
                at = slice(r, r + 32)
                near_v, far_v = levels(potentials[at], odd)
                near[at, :] = near_v[:, theirs]
                far[at, :] = far_v[:, theirs]
                parcel[at, :half] = near_v[:, theirs]
                parcel[at, half : 2 * half] = far_v[:, theirs]
                parcel[at, 2 * half : 2 * half + LANES] = near_v[:, inner]
                parcel[at, 2 * half + LANES :] = far_v[:, inner]
                rim[at, :LANES] = near_v[:, outer]
                rim[at, LANES:] = far_v[:, outer]


def cross_kernel(weights, out):
    n = out.shape[0]
    out[...] = (weights[n:, :n].astype(jnp.float32) + weights[:n, n:].astype(jnp.float32).T).astype(out.dtype)


def x_change(block):
    x = lax.rem(lax.broadcasted_iota(jnp.int32, block.shape, 1), NX)
    back = pltpu.roll(block, 2, 1)
    return jnp.where(x == 0, 0.0, block) - jnp.where(x == 1, 0.0, back)


def y_change(blocks, rim, first):
    lane = lax.broadcasted_iota(jnp.int32, rim.shape, 1)
    turned = [pltpu.roll(block, 2 * NX, 1) for block in blocks]
    above = jnp.where(first, rim, 0.0)
    below = jnp.where(first, 0.0, pltpu.roll(rim, 2 * NX, 1))
    out = []
    for b, block in enumerate(blocks):
        if b == 0:
            upper = jnp.where(lane < NX, above, block)
            lower = jnp.where(lane < NX, turned[-1], jnp.where(lane < 2 * NX, below, turned[0]))
        else:
            upper = block
            lower = jnp.where(lane < 2 * NX, turned[b - 1], turned[b])
        out.append(upper - lower)
    return out


def plane_kernel(near, far, rim, parcel, weights, cross, out, delta):
    first = spot()[1] == 0
    rows, half = near.shape
    count = half // LANES
    step = 128
    for layer, own in enumerate((near, far)):
        for group in range(2):
            for r in range(0, rows, step):
                at = pl.ds(r, step)
                if group == 0:
                    body = own[at, :]
                    edge = rim[at, layer * LANES : (layer + 1) * LANES]
                else:
                    body = parcel[at, layer * half : (layer + 1) * half]
                    edge = parcel[at, 2 * half + layer * LANES : 2 * half + (layer + 1) * LANES]
                body, edge = body.astype(jnp.float32), edge.astype(jnp.float32)
                blocks = [body[:, b * LANES : (b + 1) * LANES] for b in range(count)]
                along_y = y_change(blocks, edge, first)
                along_x = [x_change(block) for block in blocks]
                at = group * rows + r
                delta[0, at : at + step, :] = jnp.concatenate(along_y, axis=1).astype(jnp.bfloat16)
                delta[1, at : at + step, :] = jnp.concatenate(along_x, axis=1).astype(jnp.bfloat16)
        for part in range(2):
            total = jnp.zeros((8, half), jnp.float32)
            for at in range(0, 2 * rows, 256):
                grads = delta[part, at : at + 256, :]
                if at < rows:
                    mixed = dot(weights[at : at + 256, :rows], delta[part, :rows, :])
                else:
                    mixed = dot(weights[at : at + 256, rows:], delta[part, rows:, :])
                    mixed = mixed + dot(cross[at - rows : at - rows + 256, :], delta[part, :rows, :])
                total = total + jnp.sum((grads.astype(jnp.float32) * mixed).reshape(-1, 8, half), axis=0)
            total = 0.25 * jnp.sum(total, axis=0, keepdims=True)
            if part == 0:
                total = pltpu.roll(jnp.broadcast_to(total, (8, half)), half - NX, 1)
            else:
                total = jnp.broadcast_to(total, (8, half))
                total = jnp.concatenate(
                    [pltpu.roll(total[:, b * LANES : (b + 1) * LANES], LANES - 1, 1) for b in range(count)], axis=1
                )
            out[2 * layer + part : 2 * layer + part + 1, :] = total[:1]


def differences(inside, far, near_in, far_in, rows):
    near_v = near_in[rows, :].astype(jnp.float32)
    change_a = far[rows, :].astype(jnp.float32) - near_v
    change_b = jnp.where(inside, far_in[rows, :].astype(jnp.float32), 0.0) - near_v
    return change_a.astype(jnp.bfloat16), change_b.astype(jnp.bfloat16)


def early_kernel(far, near_in, far_in, weights, cross, carry_a, carry_b, out_a, out_b, delta):
    rows, half = far.shape
    inside = spot()[2]
    for r in range(0, rows, 128):
        at = pl.ds(r, 128)
        delta[at, :half], delta[at, half:] = differences(inside, far, near_in, far_in, at)
    total = jnp.zeros((8, 2 * half), jnp.float32)
    for r in range(0, rows, 256):
        mixed = dot(weights[r : r + 256, :rows], delta[...])
        carry = dot(cross[r : r + 256, :], delta[...])
        carry_a[r : r + 256, :] = carry[:, :half]
        carry_b[r : r + 256, :] = carry[:, half:]
        total = total + jnp.sum((delta[r : r + 256, :].astype(jnp.float32) * mixed).reshape(-1, 8, 2 * half), axis=0)
    out_a[...] = total[:, :half]
    out_b[...] = total[:, half:]


def close_kernel(upper, lower, weights, carry, early, out, start=0, masked=False):
    rows, half = lower.shape
    upper = upper.at[:, start : start + half]
    changes = []
    for r in range(0, rows, 128):
        above = upper[r : r + 128, :].astype(jnp.float32)
        if masked:
            above = jnp.where(spot()[2], above, 0.0)
        changes.append(above - lower[r : r + 128, :].astype(jnp.float32))
    delta = jnp.concatenate(changes, axis=0).astype(jnp.bfloat16)
    total = early[...]
    for r in range(0, rows, 256):
        mixed = carry[r : r + 256, :] + dot(weights[rows + r : rows + r + 256, rows:], delta)
        total = total + jnp.sum((delta[r : r + 256, :].astype(jnp.float32) * mixed).reshape(-1, 8, half), axis=0)
    out[...] = 0.25 * jnp.sum(total, axis=0, keepdims=True)


def assemble(quadripoles, weighted_misfit, order):
    left_side = (quadripoles[:, 0][None, :] == order[:, None]).astype(jnp.bfloat16) - (
        quadripoles[:, 1][None, :] == order[:, None]
    ).astype(jnp.bfloat16)
    third = quadripoles[:, 2][:, None] == order[None, :]
    fourth = quadripoles[:, 3][:, None] == order[None, :]
    signed = third.astype(jnp.float32) - fourth.astype(jnp.float32)
    right_side = (weighted_misfit.astype(jnp.float32)[:, None] * signed).astype(jnp.bfloat16)
    return dot(left_side, right_side).astype(jnp.bfloat16)


def local(potentials, elec_order, quadripoles, weighted_misfit, salinity, water_content, cementation, anisotropy):
    blocks = lax.axis_size("space")
    s = lax.axis_index("space")
    c = lax.axis_index("elec")
    rows, layers, cells = potentials.shape
    half = cells // 2
    odd = lax.rem(s, 2)
    to_mate = [(i, i ^ 1) for i in range(blocks)]
    ahead = [(i, (i + (2 if i % 2 else -2)) % blocks) for i in range(blocks)]
    inner = [(i, j) for i, j in ahead if abs(i - j) == 2]
    swap = [(0, 1), (1, 0)]
    low_core, near_level = c == 0, 1 - odd
    potentials, odd, c, low_core, near_level = lax.optimization_barrier((potentials, odd, c, low_core, near_level))
    shape = jax.ShapeDtypeStruct
    bf16, f32 = jnp.bfloat16, jnp.float32
    both = ("space", "elec")

    def joint(pairs, cross):
        return [(2 * i + k, 2 * j + (k ^ cross)) for i, j in pairs for k in range(2)]

    piece = shape((rows, half), bf16)
    strip = shape((rows, 2 * LANES), bf16)
    near, far = call(
        keep_kernel,
        (piece,) * 2,
        [pl.BlockSpec(memory_space=pl.ANY)],
        "keep",
        scratch=[pltpu.VMEM((rows, layers, half), bf16), pltpu.SemaphoreType.DMA((4,))],
        moved=rows * cells * 4,
        limit=FIRST,
    )(potentials)
    near_in_0 = lax.ppermute(near, both, joint(to_mate, 0))
    far_in_0 = lax.ppermute(far, both, joint(ahead, 0))
    near, far, potentials = lax.optimization_barrier((near, far, potentials))
    near_give, far_give, parcel, rim = call(
        give_kernel,
        (piece, piece, shape((rows, 2 * half + 2 * LANES), bf16), strip),
        [VMEM],
        "give",
        moved=rows * cells * 8,
        limit=4,
    )(potentials)
    parcel = lax.ppermute(parcel, "elec", swap)

    order = jnp.where(low_core, elec_order, jnp.concatenate([elec_order[rows:], elec_order[:rows]]))
    if True:
        quadripoles, near_give = lax.optimization_barrier((quadripoles, near_give))
    weights = assemble(quadripoles, weighted_misfit, order)
    cross = call(cross_kernel, shape((rows, rows), bf16), [VMEM], "cross", moved=4 * rows * rows * 2)(weights)
    near_give, weights = lax.optimization_barrier((near_give, weights))
    far_give, cross = lax.optimization_barrier((far_give, cross))
    near_in_1 = lax.ppermute(near_give, both, joint(to_mate, 1))
    far_in_1 = lax.ppermute(far_give, both, joint(inner, 1))

    big = 2 * rows * rows * half * 2
    forms = call(
        plane_kernel,
        shape((2 * layers, half), f32),
        [VMEM] * 6,
        "plane",
        scratch=[pltpu.VMEM((2, 2 * rows, half), bf16)],
        limit=16,
        flops=big * 6,
        moved=rows * cells * 16,
    )(near, far, rim, parcel, weights, cross)

    bulk = 0.15 * salinity * water_content**cementation
    salt_scale = bulk / salinity
    water_scale = bulk * cementation / water_content
    row = lax.broadcasted_iota(jnp.int32, (layers, cells), 0)
    is_near = row == near_level
    is_mine = lax.broadcasted_iota(jnp.int32, (1, cells), 1) // half == c

    def spread(near_mine, near_other, far_mine, far_other):
        def line(mine, other):
            return jnp.where(is_mine, jnp.concatenate([mine, mine], 1), jnp.concatenate([other, other], 1))

        return jnp.where(is_near, line(near_mine, near_other), line(far_mine, far_other))

    forms_x = lax.ppermute(forms, "elec", swap)
    flat = anisotropy[1] * spread(forms[0:1], forms_x[0:1], forms[2:3], forms_x[2:3])
    flat = flat + anisotropy[2] * spread(forms[1:2], forms_x[1:2], forms[3:4], forms_x[3:4])
    salt_base, water_base = salt_scale * flat, water_scale * flat
    salt_scale, water_scale = salt_scale * anisotropy[0], water_scale * anisotropy[0]

    weights_e, forms = lax.optimization_barrier((weights, forms))
    carry_a, carry_b, early_a, early_b = call(
        early_kernel,
        (shape((rows, half), f32),) * 2 + (shape((8, half), f32),) * 2,
        [VMEM] * 5,
        "early",
        scratch=[pltpu.VMEM((rows, 2 * half), bf16)],
        flops=big * 4,
        moved=rows * cells * 16,
    )(far, near_in_0, far_in_0, weights_e, cross)
    early_a, salt_base, water_base, salt_scale, water_scale = lax.optimization_barrier(
        (early_a, salt_base, water_base, salt_scale, water_scale)
    )

    def close(name, start, masked, *given):
        return call(
            functools.partial(close_kernel, start=start, masked=masked), shape((1, half), f32), [VMEM] * 5, name, flops=big, moved=rows * cells * 8, limit=6
        )(*given)

    form_a = close("close_a", half, False, parcel, near_in_1, weights, carry_a, early_a)
    a_x = lax.ppermute(form_a, "elec", swap)
    if HOLD:
        far_in_1, form_a = lax.optimization_barrier((far_in_1, form_a))
    form_b = close("close_b", 0, True, far_in_1, near_in_1, weights, carry_b, early_b)
    b_cross = lax.ppermute(form_b, both, joint(to_mate, 1))
    b_same = lax.ppermute(form_b, both, joint(to_mate, 0))
    form_z = spread(form_a, a_x, b_same, b_cross)
    return salt_scale * form_z + salt_base, water_scale * form_z + water_base


def solution(mesh):
    split = P(("slab", "space"), None)
    placed = (P("elec", ("slab", "space"), None), P(), P(), P("slab"), split, split, split, P(None, ("slab", "space"), None))
    return jax.shard_map(local, mesh=mesh, in_specs=placed, out_specs=(split, split), check_vma=False)
```

```python
import functools
import jax
import jax.numpy as jnp
from jax import lax
from jax.experimental import pallas as pl
from jax.experimental.pallas import tpu as pltpu
from jax.sharding import PartitionSpec as P

NX = 32
LANES = 128
VMEM = pl.BlockSpec(memory_space=pltpu.VMEM)
MIB = 2**20


def call(kernel, outs, specs, name, scratch=(), limit=8, flops=0, moved=0):
    return pl.pallas_call(
        kernel,
        out_shape=outs,
        in_specs=specs,
        out_specs=jax.tree.map(lambda _: VMEM, outs),
        scratch_shapes=scratch,
        compiler_params=pltpu.CompilerParams(vmem_limit_bytes=limit * MIB),
        cost_estimate=pl.CostEstimate(flops=flops, bytes_accessed=moved, transcendentals=0),
        name=name,
    )


def dot(left, right):
    return jnp.dot(left, right, preferred_element_type=jnp.float32)


def spot():
    index = lax.axis_index("space")
    odd = lax.rem(index, 2)
    inside = jnp.where(odd == 1, index >= 2, index + 2 < lax.axis_size("space"))
    return odd, lax.axis_index("elec"), inside


def levels(block, odd):
    layers = jnp.swapaxes(block, 0, 1)
    return jnp.where(odd == 1, layers[0], layers[1]), jnp.where(odd == 1, layers[1], layers[0])


def keep_kernel(potentials, near, far, raw, sems):
    odd, core, _ = spot()
    rows, half = near.shape
    size = rows // sems.shape[0]
    cells = pl.ds(pl.multiple_of(core * half, LANES), half)
    copies = []
    for i in range(sems.shape[0]):
        part = pl.ds(i * size, size)
        copies.append(pltpu.make_async_copy(potentials.at[part, :, cells], raw.at[part], sems.at[i]))
        copies[-1].start()
    for i, copy in enumerate(copies):
        copy.wait()
        for k in range(2):

            @pl.when(odd == k)
            def _():
                for r in range(i * size, (i + 1) * size, 64):
                    layers = jnp.swapaxes(raw[r : r + 64], 0, 1)
                    near[r : r + 64, :], far[r : r + 64, :] = layers[1 - k], layers[k]


def give_kernel(potentials, near, far, parcel, rim):
    odd, core, _ = spot()
    rows, half = near.shape
    for k in range(2):
        low, high = slice(half - LANES, half), slice(half, half + LANES)
        inner, outer = (low, high) if k == 0 else (high, low)
        theirs = slice((1 - k) * half, (2 - k) * half)

        @pl.when(core == k)
        def _():
            for r in range(0, rows, 32):
                at = slice(r, r + 32)
                near_v, far_v = levels(potentials[at], odd)
                near[at, :] = near_v[:, theirs]
                far[at, :] = far_v[:, theirs]
                parcel[at, :half] = near_v[:, theirs]
                parcel[at, half : 2 * half] = far_v[:, theirs]
                parcel[at, 2 * half : 2 * half + LANES] = near_v[:, inner]
                parcel[at, 2 * half + LANES :] = far_v[:, inner]
                rim[at, :LANES] = near_v[:, outer]
                rim[at, LANES:] = far_v[:, outer]


def cross_kernel(weights, out):
    n = out.shape[0]
    out[...] = (weights[n:, :n].astype(jnp.float32) + weights[:n, n:].astype(jnp.float32).T).astype(out.dtype)


def x_change(block):
    x = lax.rem(lax.broadcasted_iota(jnp.int32, block.shape, 1), NX)
    back = pltpu.roll(block, 2, 1)
    return jnp.where(x == 0, 0.0, block) - jnp.where(x == 1, 0.0, back)


def y_change(blocks, rim, first):
    lane = lax.broadcasted_iota(jnp.int32, rim.shape, 1)
    turned = [pltpu.roll(block, 2 * NX, 1) for block in blocks]
    above = jnp.where(first, rim, 0.0)
    below = jnp.where(first, 0.0, pltpu.roll(rim, 2 * NX, 1))
    out = []
    for b, block in enumerate(blocks):
        if b == 0:
            upper = jnp.where(lane < NX, above, block)
            lower = jnp.where(lane < NX, turned[-1], jnp.where(lane < 2 * NX, below, turned[0]))
        else:
            upper = block
            lower = jnp.where(lane < 2 * NX, turned[b - 1], turned[b])
        out.append(upper - lower)
    return out


def plane_kernel(near, far, rim, parcel, weights, cross, out, delta):
    first = spot()[1] == 0
    rows, half = near.shape
    count = half // LANES
    step = 128
    for layer, own in enumerate((near, far)):
        for group in range(2):
            for r in range(0, rows, step):
                at = pl.ds(r, step)
                if group == 0:
                    body = own[at, :]
                    edge = rim[at, layer * LANES : (layer + 1) * LANES]
                else:
                    body = parcel[at, layer * half : (layer + 1) * half]
                    edge = parcel[at, 2 * half + layer * LANES : 2 * half + (layer + 1) * LANES]
                body, edge = body.astype(jnp.float32), edge.astype(jnp.float32)
                blocks = [body[:, b * LANES : (b + 1) * LANES] for b in range(count)]
                along_y = y_change(blocks, edge, first)
                along_x = [x_change(block) for block in blocks]
                at = group * rows + r
                delta[0, at : at + step, :] = jnp.concatenate(along_y, axis=1).astype(jnp.bfloat16)
                delta[1, at : at + step, :] = jnp.concatenate(along_x, axis=1).astype(jnp.bfloat16)
        for part in range(2):
            total = jnp.zeros((8, half), jnp.float32)
            for at in range(0, 2 * rows, 256):
                grads = delta[part, at : at + 256, :]
                if at < rows:
                    mixed = dot(weights[at : at + 256, :rows], delta[part, :rows, :])
                else:
                    mixed = dot(weights[at : at + 256, rows:], delta[part, rows:, :])
                    mixed = mixed + dot(cross[at - rows : at - rows + 256, :], delta[part, :rows, :])
                total = total + jnp.sum((grads.astype(jnp.float32) * mixed).reshape(-1, 8, half), axis=0)
            total = 0.25 * jnp.sum(total, axis=0, keepdims=True)
            if part == 0:
                total = pltpu.roll(jnp.broadcast_to(total, (8, half)), half - NX, 1)
            else:
                total = jnp.broadcast_to(total, (8, half))
                total = jnp.concatenate(
                    [pltpu.roll(total[:, b * LANES : (b + 1) * LANES], LANES - 1, 1) for b in range(count)], axis=1
                )
            out[2 * layer + part : 2 * layer + part + 1, :] = total[:1]


def differences(inside, far, near_in, far_in, rows):
    near_v = near_in[rows, :].astype(jnp.float32)
    change_a = far[rows, :].astype(jnp.float32) - near_v
    change_b = jnp.where(inside, far_in[rows, :].astype(jnp.float32), 0.0) - near_v
    return change_a.astype(jnp.bfloat16), change_b.astype(jnp.bfloat16)


def early_kernel(far, near_in, far_in, weights, cross, carry_a, carry_b, out_a, out_b, delta):
    rows, half = far.shape
    inside = spot()[2]
    for r in range(0, rows, 128):
        at = pl.ds(r, 128)
        delta[at, :half], delta[at, half:] = differences(inside, far, near_in, far_in, at)
    total = jnp.zeros((8, 2 * half), jnp.float32)
    for r in range(0, rows, 256):
        mixed = dot(weights[r : r + 256, :rows], delta[...])
        carry = dot(cross[r : r + 256, :], delta[...])
        carry_a[r : r + 256, :] = carry[:, :half]
        carry_b[r : r + 256, :] = carry[:, half:]
        total = total + jnp.sum((delta[r : r + 256, :].astype(jnp.float32) * mixed).reshape(-1, 8, 2 * half), axis=0)
    out_a[...] = total[:, :half]
    out_b[...] = total[:, half:]


def close_kernel(upper, lower, weights, carry, early, out, start=0, masked=False):
    rows, half = lower.shape
    inside = spot()[2]
    wide = half // 2
    for c in range(0, half, wide):
        changes = []
        for r in range(0, rows, 128):
            above = upper[r : r + 128, start + c : start + c + wide].astype(jnp.float32)
            if masked:
                above = jnp.where(inside, above, 0.0)
            changes.append((above - lower[r : r + 128, c : c + wide].astype(jnp.float32)).astype(jnp.bfloat16))
        delta = jnp.concatenate(changes, axis=0)
        total = early[:, c : c + wide]
        for r in range(0, rows, 256):
            mixed = carry[r : r + 256, c : c + wide] + dot(weights[rows + r : rows + r + 256, rows:], delta)
            total = total + jnp.sum((delta[r : r + 256, :].astype(jnp.float32) * mixed).reshape(-1, 8, wide), axis=0)
        out[:, c : c + wide] = 0.25 * jnp.sum(total, axis=0, keepdims=True)


def assemble(quadripoles, weighted_misfit, order):
    left_side = (quadripoles[:, 0][None, :] == order[:, None]).astype(jnp.bfloat16) - (
        quadripoles[:, 1][None, :] == order[:, None]
    ).astype(jnp.bfloat16)
    third = quadripoles[:, 2][:, None] == order[None, :]
    fourth = quadripoles[:, 3][:, None] == order[None, :]
    signed = third.astype(jnp.float32) - fourth.astype(jnp.float32)
    right_side = (weighted_misfit.astype(jnp.float32)[:, None] * signed).astype(jnp.bfloat16)
    return dot(left_side, right_side).astype(jnp.bfloat16)


def local(potentials, elec_order, quadripoles, weighted_misfit, salinity, water_content, cementation, anisotropy):
    blocks = lax.axis_size("space")
    s = lax.axis_index("space")
    c = lax.axis_index("elec")
    rows, layers, cells = potentials.shape
    half = cells // 2
    odd = lax.rem(s, 2)
    to_mate = [(i, i ^ 1) for i in range(blocks)]
    ahead = [(i, (i + (2 if i % 2 else -2)) % blocks) for i in range(blocks)]
    inner = [(i, j) for i, j in ahead if abs(i - j) == 2]
    swap = [(0, 1), (1, 0)]
    low_core, near_level = c == 0, 1 - odd
    potentials, odd, c, low_core, near_level = lax.optimization_barrier((potentials, odd, c, low_core, near_level))
    shape = jax.ShapeDtypeStruct
    bf16, f32 = jnp.bfloat16, jnp.float32
    both = ("space", "elec")

    def joint(pairs, cross):
        return [(2 * i + k, 2 * j + (k ^ cross)) for i, j in pairs for k in range(2)]

    piece = shape((rows, half), bf16)
    strip = shape((rows, 2 * LANES), bf16)
    near, far = call(
        keep_kernel,
        (piece,) * 2,
        [pl.BlockSpec(memory_space=pl.ANY)],
        "keep",
        scratch=[pltpu.VMEM((rows, layers, half), bf16), pltpu.SemaphoreType.DMA((4,))],
        moved=rows * cells * 4,
        limit=51,
    )(potentials)
    near_in_0 = lax.ppermute(near, both, joint(to_mate, 0))
    far_in_0 = lax.ppermute(far, both, joint(ahead, 0))
    near, far, potentials = lax.optimization_barrier((near, far, potentials))
    near_give, far_give, parcel, rim = call(
        give_kernel,
        (piece, piece, shape((rows, 2 * half + 2 * LANES), bf16), strip),
        [VMEM],
        "give",
        moved=rows * cells * 8,
        limit=4,
    )(potentials)
    parcel = lax.ppermute(parcel, "elec", swap)

    order = jnp.where(low_core, elec_order, jnp.concatenate([elec_order[rows:], elec_order[:rows]]))
    quadripoles, near_give = lax.optimization_barrier((quadripoles, near_give))
    weights = assemble(quadripoles, weighted_misfit, order)
    cross = call(cross_kernel, shape((rows, rows), bf16), [VMEM], "cross", moved=4 * rows * rows * 2)(weights)
    near_give, weights = lax.optimization_barrier((near_give, weights))
    far_give, cross = lax.optimization_barrier((far_give, cross))
    near_in_1 = lax.ppermute(near_give, both, joint(to_mate, 1))
    far_in_1 = lax.ppermute(far_give, both, joint(inner, 1))

    big = 2 * rows * rows * half * 2
    forms = call(
        plane_kernel,
        shape((2 * layers, half), f32),
        [VMEM] * 6,
        "plane",
        scratch=[pltpu.VMEM((2, 2 * rows, half), bf16)],
        limit=16,
        flops=big * 6,
        moved=rows * cells * 16,
    )(near, far, rim, parcel, weights, cross)

    bulk = 0.15 * salinity * water_content**cementation
    salt_scale = bulk / salinity
    water_scale = bulk * cementation / water_content
    row = lax.broadcasted_iota(jnp.int32, (layers, cells), 0)
    is_near = row == near_level
    is_mine = lax.broadcasted_iota(jnp.int32, (1, cells), 1) // half == c

    def spread(near_mine, near_other, far_mine, far_other):
        def line(mine, other):
            return jnp.where(is_mine, jnp.concatenate([mine, mine], 1), jnp.concatenate([other, other], 1))

        return jnp.where(is_near, line(near_mine, near_other), line(far_mine, far_other))

    forms_x = lax.ppermute(forms, "elec", swap)
    flat = anisotropy[1] * spread(forms[0:1], forms_x[0:1], forms[2:3], forms_x[2:3])
    flat = flat + anisotropy[2] * spread(forms[1:2], forms_x[1:2], forms[3:4], forms_x[3:4])
    salt_base, water_base = salt_scale * flat, water_scale * flat
    salt_scale, water_scale = salt_scale * anisotropy[0], water_scale * anisotropy[0]

    weights_e, forms = lax.optimization_barrier((weights, forms))
    carry_a, carry_b, early_a, early_b = call(
        early_kernel,
        (shape((rows, half), f32),) * 2 + (shape((8, half), f32),) * 2,
        [VMEM] * 5,
        "early",
        scratch=[pltpu.VMEM((rows, 2 * half), bf16)],
        flops=big * 4,
        moved=rows * cells * 16,
    )(far, near_in_0, far_in_0, weights_e, cross)
    early_a, salt_base, water_base, salt_scale, water_scale = lax.optimization_barrier(
        (early_a, salt_base, water_base, salt_scale, water_scale)
    )

    def close(name, start, masked, *given):
        return call(
            functools.partial(close_kernel, start=start, masked=masked), shape((1, half), f32), [VMEM] * 5, name, flops=big, moved=rows * cells * 8, limit=6
        )(*given)

    form_a = close("close_a", half, False, parcel, near_in_1, weights, carry_a, early_a)
    a_x = lax.ppermute(form_a, "elec", swap)
    far_in_1, form_a = lax.optimization_barrier((far_in_1, form_a))
    form_b = close("close_b", 0, True, far_in_1, near_in_1, weights, carry_b, early_b)
    b_cross = lax.ppermute(form_b, both, joint(to_mate, 1))
    b_same = lax.ppermute(form_b, both, joint(to_mate, 0))
    form_z = spread(form_a, a_x, b_same, b_cross)
    return salt_scale * form_z + salt_base, water_scale * form_z + water_base


def solution(mesh):
    split = P(("slab", "space"), None)
    placed = (P("elec", ("slab", "space"), None), P(), P(), P("slab"), split, split, split, P(None, ("slab", "space"), None))
    return jax.shard_map(local, mesh=mesh, in_specs=placed, out_specs=(split, split), check_vma=False)
```

```python
import functools
import jax
import jax.numpy as jnp
from jax import lax
from jax.experimental import pallas as pl
from jax.experimental.pallas import tpu as pltpu
from jax.sharding import PartitionSpec as P

NX = 32
LANES = 128
VMEM = pl.BlockSpec(memory_space=pltpu.VMEM)
MIB = 2**20


def call(kernel, outs, specs, name, scratch=(), limit=8, flops=0, moved=0):
    return pl.pallas_call(
        kernel,
        out_shape=outs,
        in_specs=specs,
        out_specs=jax.tree.map(lambda _: VMEM, outs),
        scratch_shapes=scratch,
        compiler_params=pltpu.CompilerParams(vmem_limit_bytes=limit * MIB),
        cost_estimate=pl.CostEstimate(flops=flops, bytes_accessed=moved, transcendentals=0),
        name=name,
    )


def dot(left, right):
    return jnp.dot(left, right, preferred_element_type=jnp.float32)


def spot():
    index = lax.axis_index("space")
    odd = lax.rem(index, 2)
    inside = jnp.where(odd == 1, index >= 2, index + 2 < lax.axis_size("space"))
    return odd, lax.axis_index("elec"), inside


def levels(block, odd):
    layers = jnp.swapaxes(block, 0, 1)
    return jnp.where(odd == 1, layers[0], layers[1]), jnp.where(odd == 1, layers[1], layers[0])


def keep_kernel(potentials, near, far, raw, sems):
    odd, core, _ = spot()
    rows, half = near.shape
    size = rows // sems.shape[0]
    cells = pl.ds(pl.multiple_of(core * half, LANES), half)
    copies = []
    for i in range(sems.shape[0]):
        part = pl.ds(i * size, size)
        copies.append(pltpu.make_async_copy(potentials.at[part, :, cells], raw.at[part], sems.at[i]))
        copies[-1].start()
    for i, copy in enumerate(copies):
        copy.wait()
        for k in range(2):

            @pl.when(odd == k)
            def _():
                for r in range(i * size, (i + 1) * size, 64):
                    layers = jnp.swapaxes(raw[r : r + 64], 0, 1)
                    near[r : r + 64, :], far[r : r + 64, :] = layers[1 - k], layers[k]


def give_kernel(potentials, near, far, parcel, rim):
    odd, core, _ = spot()
    rows, half = near.shape
    for k in range(2):
        low, high = slice(half - LANES, half), slice(half, half + LANES)
        inner, outer = (low, high) if k == 0 else (high, low)
        theirs = slice((1 - k) * half, (2 - k) * half)

        @pl.when(core == k)
        def _():
            for r in range(0, rows, 32):
                at = slice(r, r + 32)
                near_v, far_v = levels(potentials[at], odd)
                near[at, :] = near_v[:, theirs]
                far[at, :] = far_v[:, theirs]
                parcel[at, :half] = near_v[:, theirs]
                parcel[at, half : 2 * half] = far_v[:, theirs]
                parcel[at, 2 * half : 2 * half + LANES] = near_v[:, inner]
                parcel[at, 2 * half + LANES :] = far_v[:, inner]
                rim[at, :LANES] = near_v[:, outer]
                rim[at, LANES:] = far_v[:, outer]


def cross_kernel(weights, out):
    n = out.shape[0]
    out[...] = (weights[n:, :n].astype(jnp.float32) + weights[:n, n:].astype(jnp.float32).T).astype(out.dtype)


def x_change(block):
    x = lax.rem(lax.broadcasted_iota(jnp.int32, block.shape, 1), NX)
    back = pltpu.roll(block, 2, 1)
    return jnp.where(x == 0, 0.0, block) - jnp.where(x == 1, 0.0, back)


def y_change(blocks, rim, first):
    lane = lax.broadcasted_iota(jnp.int32, rim.shape, 1)
    turned = [pltpu.roll(block, 2 * NX, 1) for block in blocks]
    above = jnp.where(first, rim, 0.0)
    below = jnp.where(first, 0.0, pltpu.roll(rim, 2 * NX, 1))
    out = []
    for b, block in enumerate(blocks):
        if b == 0:
            upper = jnp.where(lane < NX, above, block)
            lower = jnp.where(lane < NX, turned[-1], jnp.where(lane < 2 * NX, below, turned[0]))
        else:
            upper = block
            lower = jnp.where(lane < 2 * NX, turned[b - 1], turned[b])
        out.append(upper - lower)
    return out


def plane_kernel(near, far, rim, parcel, weights, cross, out, delta):
    first = spot()[1] == 0
    rows, half = near.shape
    count = half // LANES
    step = 128
    for layer, own in enumerate((near, far)):
        for group in range(2):
            for r in range(0, rows, step):
                at = pl.ds(r, step)
                if group == 0:
                    body = own[at, :]
                    edge = rim[at, layer * LANES : (layer + 1) * LANES]
                else:
                    body = parcel[at, layer * half : (layer + 1) * half]
                    edge = parcel[at, 2 * half + layer * LANES : 2 * half + (layer + 1) * LANES]
                body, edge = body.astype(jnp.float32), edge.astype(jnp.float32)
                blocks = [body[:, b * LANES : (b + 1) * LANES] for b in range(count)]
                along_y = y_change(blocks, edge, first)
                along_x = [x_change(block) for block in blocks]
                at = group * rows + r
                delta[0, at : at + step, :] = jnp.concatenate(along_y, axis=1).astype(jnp.bfloat16)
                delta[1, at : at + step, :] = jnp.concatenate(along_x, axis=1).astype(jnp.bfloat16)
        for part in range(2):
            total = jnp.zeros((8, half), jnp.float32)
            for at in range(0, 2 * rows, 256):
                grads = delta[part, at : at + 256, :]
                if at < rows:
                    mixed = dot(weights[at : at + 256, :rows], delta[part, :rows, :])
                else:
                    mixed = dot(weights[at : at + 256, rows:], delta[part, rows:, :])
                    mixed = mixed + dot(cross[at - rows : at - rows + 256, :], delta[part, :rows, :])
                total = total + jnp.sum((grads.astype(jnp.float32) * mixed).reshape(-1, 8, half), axis=0)
            total = 0.25 * jnp.sum(total, axis=0, keepdims=True)
            if part == 0:
                total = pltpu.roll(jnp.broadcast_to(total, (8, half)), half - NX, 1)
            else:
                total = jnp.broadcast_to(total, (8, half))
                total = jnp.concatenate(
                    [pltpu.roll(total[:, b * LANES : (b + 1) * LANES], LANES - 1, 1) for b in range(count)], axis=1
                )
            out[2 * layer + part : 2 * layer + part + 1, :] = total[:1]


def differences(inside, far, near_in, far_in, rows):
    near_v = near_in[rows, :].astype(jnp.float32)
    change_a = far[rows, :].astype(jnp.float32) - near_v
    change_b = jnp.where(inside, far_in[rows, :].astype(jnp.float32), 0.0) - near_v
    return change_a.astype(jnp.bfloat16), change_b.astype(jnp.bfloat16)


def early_kernel(far, near_in, far_in, weights, cross, carry_a, carry_b, out_a, out_b, delta):
    rows, half = far.shape
    inside = spot()[2]
    for r in range(0, rows, 128):
        at = pl.ds(r, 128)
        delta[at, :half], delta[at, half:] = differences(inside, far, near_in, far_in, at)
    total = jnp.zeros((8, 2 * half), jnp.float32)
    for r in range(0, rows, 256):
        mixed = dot(weights[r : r + 256, :rows], delta[...])
        carry = dot(cross[r : r + 256, :], delta[...])
        carry_a[r : r + 256, :] = carry[:, :half]
        carry_b[r : r + 256, :] = carry[:, half:]
        total = total + jnp.sum((delta[r : r + 256, :].astype(jnp.float32) * mixed).reshape(-1, 8, 2 * half), axis=0)
    out_a[...] = total[:, :half]
    out_b[...] = total[:, half:]


def close_kernel(upper, lower, weights, carry, early, out, start=0, masked=False):
    rows, half = lower.shape
    inside = spot()[2]
    wide = half // 2
    for c in range(0, half, wide):
        changes = []
        for r in range(0, rows, 128):
            above = upper[r : r + 128, start + c : start + c + wide].astype(jnp.float32)
            if masked:
                above = jnp.where(inside, above, 0.0)
            changes.append((above - lower[r : r + 128, c : c + wide].astype(jnp.float32)).astype(jnp.bfloat16))
        delta = jnp.concatenate(changes, axis=0)
        mixed = carry[:, c : c + wide] + dot(weights[rows:, rows:], delta)
        total = early[:, c : c + wide] + jnp.sum((delta.astype(jnp.float32) * mixed).reshape(-1, 8, wide), axis=0)
        out[:, c : c + wide] = 0.25 * jnp.sum(total, axis=0, keepdims=True)


def finish_kernel(b, b_x, a_x, a, salt_scale, salt_base, water_scale, water_base, salt, water):
    odd, core, _ = spot()
    half = a.shape[1]
    for k in range(2):
        for n in range(2):

            @pl.when((odd == n) & (core == k))
            def _():
                for mine, other, row in ((a, a_x, 1 - n), (b, b_x, n)):
                    for value, side in ((mine, k), (other, 1 - k)):
                        at = (slice(row, row + 1), slice(side * half, (side + 1) * half))
                        salt[at] = salt_scale[at] * value[...] + salt_base[at]
                        water[at] = water_scale[at] * value[...] + water_base[at]


def assemble(quadripoles, weighted_misfit, order):
    left_side = (quadripoles[:, 0][None, :] == order[:, None]).astype(jnp.bfloat16) - (
        quadripoles[:, 1][None, :] == order[:, None]
    ).astype(jnp.bfloat16)
    third = quadripoles[:, 2][:, None] == order[None, :]
    fourth = quadripoles[:, 3][:, None] == order[None, :]
    signed = third.astype(jnp.float32) - fourth.astype(jnp.float32)
    right_side = (weighted_misfit.astype(jnp.float32)[:, None] * signed).astype(jnp.bfloat16)
    return dot(left_side, right_side).astype(jnp.bfloat16)


def local(potentials, elec_order, quadripoles, weighted_misfit, salinity, water_content, cementation, anisotropy):
    blocks = lax.axis_size("space")
    s = lax.axis_index("space")
    c = lax.axis_index("elec")
    rows, layers, cells = potentials.shape
    half = cells // 2
    odd = lax.rem(s, 2)
    to_mate = [(i, i ^ 1) for i in range(blocks)]
    ahead = [(i, (i + (2 if i % 2 else -2)) % blocks) for i in range(blocks)]
    inner = [(i, j) for i, j in ahead if abs(i - j) == 2]
    swap = [(0, 1), (1, 0)]
    low_core, near_level = c == 0, 1 - odd
    potentials, odd, c, low_core, near_level = lax.optimization_barrier((potentials, odd, c, low_core, near_level))
    shape = jax.ShapeDtypeStruct
    bf16, f32 = jnp.bfloat16, jnp.float32
    both = ("space", "elec")

    def joint(pairs, cross):
        return [(2 * i + k, 2 * j + (k ^ cross)) for i, j in pairs for k in range(2)]

    piece = shape((rows, half), bf16)
    strip = shape((rows, 2 * LANES), bf16)
    near, far = call(
        keep_kernel,
        (piece,) * 2,
        [pl.BlockSpec(memory_space=pl.ANY)],
        "keep",
        scratch=[pltpu.VMEM((rows, layers, half), bf16), pltpu.SemaphoreType.DMA((4,))],
        moved=rows * cells * 4,
        limit=51,
    )(potentials)
    near_in_0 = lax.ppermute(near, both, joint(to_mate, 0))
    far_in_0 = lax.ppermute(far, both, joint(ahead, 0))
    near, far, potentials = lax.optimization_barrier((near, far, potentials))
    near_give, far_give, parcel, rim = call(
        give_kernel,
        (piece, piece, shape((rows, 2 * half + 2 * LANES), bf16), strip),
        [VMEM],
        "give",
        moved=rows * cells * 8,
        limit=4,
    )(potentials)
    parcel = lax.ppermute(parcel, "elec", swap)

    order = jnp.where(low_core, elec_order, jnp.concatenate([elec_order[rows:], elec_order[:rows]]))
    quadripoles, near_give = lax.optimization_barrier((quadripoles, near_give))
    weights = assemble(quadripoles, weighted_misfit, order)
    cross = call(cross_kernel, shape((rows, rows), bf16), [VMEM], "cross", moved=4 * rows * rows * 2)(weights)
    near_give, weights = lax.optimization_barrier((near_give, weights))
    far_give, cross = lax.optimization_barrier((far_give, cross))
    far_in_1 = lax.ppermute(far_give, both, joint(inner, 1))
    near_in_1 = lax.ppermute(near_give, both, joint(to_mate, 1))

    big = 2 * rows * rows * half * 2
    forms = call(
        plane_kernel,
        shape((2 * layers, half), f32),
        [VMEM] * 6,
        "plane",
        scratch=[pltpu.VMEM((2, 2 * rows, half), bf16)],
        limit=16,
        flops=big * 6,
        moved=rows * cells * 16,
    )(near, far, rim, parcel, weights, cross)

    bulk = 0.15 * salinity * water_content**cementation
    salt_scale = bulk / salinity
    water_scale = bulk * cementation / water_content
    row = lax.broadcasted_iota(jnp.int32, (layers, cells), 0)
    is_near = row == near_level
    is_mine = lax.broadcasted_iota(jnp.int32, (1, cells), 1) // half == c

    def spread(near_mine, near_other, far_mine, far_other):
        def line(mine, other):
            return jnp.where(is_mine, jnp.concatenate([mine, mine], 1), jnp.concatenate([other, other], 1))

        return jnp.where(is_near, line(near_mine, near_other), line(far_mine, far_other))

    forms_x = lax.ppermute(forms, "elec", swap)
    flat = anisotropy[1] * spread(forms[0:1], forms_x[0:1], forms[2:3], forms_x[2:3])
    flat = flat + anisotropy[2] * spread(forms[1:2], forms_x[1:2], forms[3:4], forms_x[3:4])
    salt_base, water_base = salt_scale * flat, water_scale * flat
    salt_scale, water_scale = salt_scale * anisotropy[0], water_scale * anisotropy[0]

    weights_e, forms = lax.optimization_barrier((weights, forms))
    carry_a, carry_b, early_a, early_b = call(
        early_kernel,
        (shape((rows, half), f32),) * 2 + (shape((8, half), f32),) * 2,
        [VMEM] * 5,
        "early",
        scratch=[pltpu.VMEM((rows, 2 * half), bf16)],
        flops=big * 4,
        moved=rows * cells * 16,
    )(far, near_in_0, far_in_0, weights_e, cross)
    early_a, salt_base, water_base, salt_scale, water_scale = lax.optimization_barrier(
        (early_a, salt_base, water_base, salt_scale, water_scale)
    )

    def close(name, start, masked, *given):
        return call(
            functools.partial(close_kernel, start=start, masked=masked), shape((1, half), f32), [VMEM] * 5, name, flops=big, moved=rows * cells * 8, limit=6
        )(*given)

    form_a = close("close_a", half, False, parcel, near_in_1, weights, carry_a, early_a)
    a_x = lax.ppermute(form_a, "elec", swap)
    far_in_1, form_a = lax.optimization_barrier((far_in_1, form_a))
    form_b = close("close_b", 0, True, far_in_1, near_in_1, weights, carry_b, early_b)
    b_same = lax.ppermute(form_b, both, joint(to_mate, 0))
    b_cross = lax.ppermute(form_b, both, joint(to_mate, 1))
    done = shape((layers, cells), f32)
    return pl.pallas_call(
        finish_kernel,
        out_shape=(done, done),
        in_specs=[VMEM] * 8,
        compiler_params=pltpu.CompilerParams(vmem_limit_bytes=2 * MIB),
        cost_estimate=pl.CostEstimate(flops=0, bytes_accessed=cells * 64, transcendentals=0),
        name="finish",
    )(b_same, b_cross, a_x, form_a, salt_scale, salt_base, water_scale, water_base)


def solution(mesh):
    split = P(("slab", "space"), None)
    placed = (P("elec", ("slab", "space"), None), P(), P(), P("slab"), split, split, split, P(None, ("slab", "space"), None))
    return jax.shard_map(local, mesh=mesh, in_specs=placed, out_specs=(split, split), check_vma=False)
```

```python
import functools
import jax
import jax.numpy as jnp
from jax import lax
from jax.experimental import pallas as pl
from jax.experimental.pallas import tpu as pltpu
from jax.sharding import PartitionSpec as P

NX = 32
LANES = 128
VMEM = pl.BlockSpec(memory_space=pltpu.VMEM)
MIB = 2**20


def call(kernel, outs, specs, name, scratch=(), limit=8, flops=0, moved=0):
    return pl.pallas_call(
        kernel,
        out_shape=outs,
        in_specs=specs,
        out_specs=jax.tree.map(lambda _: VMEM, outs),
        scratch_shapes=scratch,
        compiler_params=pltpu.CompilerParams(vmem_limit_bytes=limit * MIB),
        cost_estimate=pl.CostEstimate(flops=flops, bytes_accessed=moved, transcendentals=0),
        name=name,
    )


def dot(left, right):
    return jnp.dot(left, right, preferred_element_type=jnp.float32)


def spot():
    index = lax.axis_index("space")
    odd = lax.rem(index, 2)
    inside = jnp.where(odd == 1, index >= 2, index + 2 < lax.axis_size("space"))
    return odd, lax.axis_index("elec"), inside


def levels(block, odd):
    layers = jnp.swapaxes(block, 0, 1)
    return jnp.where(odd == 1, layers[0], layers[1]), jnp.where(odd == 1, layers[1], layers[0])


def keep_kernel(potentials, near, far, raw, sems):
    odd, core, _ = spot()
    rows, half = near.shape
    size = rows // sems.shape[0]
    cells = pl.ds(pl.multiple_of(core * half, LANES), half)
    copies = []
    for i in range(sems.shape[0]):
        part = pl.ds(i * size, size)
        copies.append(pltpu.make_async_copy(potentials.at[part, :, cells], raw.at[part], sems.at[i]))
        copies[-1].start()
    for i, copy in enumerate(copies):
        copy.wait()
        for k in range(2):

            @pl.when(odd == k)
            def _():
                for r in range(i * size, (i + 1) * size, 64):
                    layers = jnp.swapaxes(raw[r : r + 64], 0, 1)
                    near[r : r + 64, :], far[r : r + 64, :] = layers[1 - k], layers[k]


def give_kernel(potentials, near, far, parcel, rim, raw, sems):
    odd, core, _ = spot()
    rows, half = near.shape
    size = rows // sems.shape[0]
    copies = []
    for i in range(sems.shape[0]):
        part = pl.ds(i * size, size)
        copies.append(pltpu.make_async_copy(potentials.at[part], raw.at[part], sems.at[i]))
        copies[-1].start()
    for copy in copies:
        copy.wait()
    for k in range(2):
        low, high = slice(half - LANES, half), slice(half, half + LANES)
        inner, outer = (low, high) if k == 0 else (high, low)
        theirs = slice((1 - k) * half, (2 - k) * half)

        @pl.when(core == k)
        def _():
            for r in range(0, rows, 32):
                at = slice(r, r + 32)
                near_v, far_v = levels(raw[at], odd)
                near[at, :] = near_v[:, theirs]
                far[at, :] = far_v[:, theirs]
                parcel[at, :half] = near_v[:, theirs]
                parcel[at, half : 2 * half] = far_v[:, theirs]
                parcel[at, 2 * half : 2 * half + LANES] = near_v[:, inner]
                parcel[at, 2 * half + LANES :] = far_v[:, inner]
                rim[at, :LANES] = near_v[:, outer]
                rim[at, LANES:] = far_v[:, outer]


def cross_kernel(weights, out):
    n = out.shape[0]
    out[...] = (weights[n:, :n].astype(jnp.float32) + weights[:n, n:].astype(jnp.float32).T).astype(out.dtype)


def x_change(block):
    x = lax.rem(lax.broadcasted_iota(jnp.int32, block.shape, 1), NX)
    back = pltpu.roll(block, 2, 1)
    return jnp.where(x == 0, 0.0, block) - jnp.where(x == 1, 0.0, back)


def y_change(blocks, rim, first):
    lane = lax.broadcasted_iota(jnp.int32, rim.shape, 1)
    turned = [pltpu.roll(block, 2 * NX, 1) for block in blocks]
    above = jnp.where(first, rim, 0.0)
    below = jnp.where(first, 0.0, pltpu.roll(rim, 2 * NX, 1))
    out = []
    for b, block in enumerate(blocks):
        if b == 0:
            upper = jnp.where(lane < NX, above, block)
            lower = jnp.where(lane < NX, turned[-1], jnp.where(lane < 2 * NX, below, turned[0]))
        else:
            upper = block
            lower = jnp.where(lane < 2 * NX, turned[b - 1], turned[b])
        out.append(upper - lower)
    return out


def plane_kernel(near, far, rim, parcel, weights, cross, out, delta):
    first = spot()[1] == 0
    rows, half = near.shape
    count = half // LANES
    step = 128
    for layer, own in enumerate((near, far)):
        for group in range(2):
            for r in range(0, rows, step):
                at = pl.ds(r, step)
                if group == 0:
                    body = own[at, :]
                    edge = rim[at, layer * LANES : (layer + 1) * LANES]
                else:
                    body = parcel[at, layer * half : (layer + 1) * half]
                    edge = parcel[at, 2 * half + layer * LANES : 2 * half + (layer + 1) * LANES]
                body, edge = body.astype(jnp.float32), edge.astype(jnp.float32)
                blocks = [body[:, b * LANES : (b + 1) * LANES] for b in range(count)]
                along_y = y_change(blocks, edge, first)
                along_x = [x_change(block) for block in blocks]
                at = group * rows + r
                delta[0, at : at + step, :] = jnp.concatenate(along_y, axis=1).astype(jnp.bfloat16)
                delta[1, at : at + step, :] = jnp.concatenate(along_x, axis=1).astype(jnp.bfloat16)
        for part in range(2):
            total = jnp.zeros((8, half), jnp.float32)
            for at in range(0, 2 * rows, 256):
                grads = delta[part, at : at + 256, :]
                if at < rows:
                    mixed = dot(weights[at : at + 256, :rows], delta[part, :rows, :])
                else:
                    mixed = dot(weights[at : at + 256, rows:], delta[part, rows:, :])
                    mixed = mixed + dot(cross[at - rows : at - rows + 256, :], delta[part, :rows, :])
                total = total + jnp.sum((grads.astype(jnp.float32) * mixed).reshape(-1, 8, half), axis=0)
            total = 0.25 * jnp.sum(total, axis=0, keepdims=True)
            if part == 0:
                total = pltpu.roll(jnp.broadcast_to(total, (8, half)), half - NX, 1)
            else:
                total = jnp.broadcast_to(total, (8, half))
                total = jnp.concatenate(
                    [pltpu.roll(total[:, b * LANES : (b + 1) * LANES], LANES - 1, 1) for b in range(count)], axis=1
                )
            out[2 * layer + part : 2 * layer + part + 1, :] = total[:1]


def differences(inside, far, near_in, far_in, rows):
    near_v = near_in[rows, :].astype(jnp.float32)
    change_a = far[rows, :].astype(jnp.float32) - near_v
    change_b = jnp.where(inside, far_in[rows, :].astype(jnp.float32), 0.0) - near_v
    return change_a.astype(jnp.bfloat16), change_b.astype(jnp.bfloat16)


def early_kernel(far, near_in, far_in, weights, cross, carry_a, carry_b, out_a, out_b, delta):
    rows, half = far.shape
    inside = spot()[2]
    for r in range(0, rows, 128):
        at = pl.ds(r, 128)
        delta[at, :half], delta[at, half:] = differences(inside, far, near_in, far_in, at)
    total = jnp.zeros((8, 2 * half), jnp.float32)
    for r in range(0, rows, 256):
        mixed = dot(weights[r : r + 256, :rows], delta[...])
        carry = dot(cross[r : r + 256, :], delta[...])
        carry_a[r : r + 256, :] = carry[:, :half]
        carry_b[r : r + 256, :] = carry[:, half:]
        total = total + jnp.sum((delta[r : r + 256, :].astype(jnp.float32) * mixed).reshape(-1, 8, 2 * half), axis=0)
    out_a[...] = total[:, :half]
    out_b[...] = total[:, half:]


def close_kernel(upper, lower, weights, carry, early, out, start=0, masked=False):
    rows, half = lower.shape
    inside = spot()[2]
    wide = half // 2
    for c in range(0, half, wide):
        changes = []
        for r in range(0, rows, 128):
            above = upper[r : r + 128, start + c : start + c + wide]
            if masked:
                above = jnp.where(inside, above, jnp.zeros_like(above))
            changes.append(above - lower[r : r + 128, c : c + wide])
        delta = jnp.concatenate(changes, axis=0)
        mixed = carry[:, c : c + wide] + dot(weights[rows:, rows:], delta)
        total = early[:, c : c + wide] + jnp.sum((delta.astype(jnp.float32) * mixed).reshape(-1, 8, wide), axis=0)
        out[:, c : c + wide] = 0.25 * jnp.sum(total, axis=0, keepdims=True)


def finish_kernel(b, b_x, a_x, a, salt_scale, salt_base, water_scale, water_base, salt, water):
    odd, core, _ = spot()
    half = a.shape[1]
    for k in range(2):
        for n in range(2):

            @pl.when((odd == n) & (core == k))
            def _():
                for mine, other, row in ((a, a_x, 1 - n), (b, b_x, n)):
                    for value, side in ((mine, k), (other, 1 - k)):
                        at = (slice(row, row + 1), slice(side * half, (side + 1) * half))
                        salt[at] = salt_scale[at] * value[...] + salt_base[at]
                        water[at] = water_scale[at] * value[...] + water_base[at]


def assemble(quadripoles, weighted_misfit, order):
    left_side = (quadripoles[:, 0][None, :] == order[:, None]).astype(jnp.bfloat16) - (
        quadripoles[:, 1][None, :] == order[:, None]
    ).astype(jnp.bfloat16)
    third = quadripoles[:, 2][:, None] == order[None, :]
    fourth = quadripoles[:, 3][:, None] == order[None, :]
    signed = third.astype(jnp.float32) - fourth.astype(jnp.float32)
    right_side = (weighted_misfit.astype(jnp.float32)[:, None] * signed).astype(jnp.bfloat16)
    return dot(left_side, right_side).astype(jnp.bfloat16)


def local(potentials, elec_order, quadripoles, weighted_misfit, salinity, water_content, cementation, anisotropy):
    blocks = lax.axis_size("space")
    s = lax.axis_index("space")
    c = lax.axis_index("elec")
    rows, layers, cells = potentials.shape
    half = cells // 2
    odd = lax.rem(s, 2)
    to_mate = [(i, i ^ 1) for i in range(blocks)]
    ahead = [(i, (i + (2 if i % 2 else -2)) % blocks) for i in range(blocks)]
    inner = [(i, j) for i, j in ahead if abs(i - j) == 2]
    swap = [(0, 1), (1, 0)]
    low_core, near_level = c == 0, 1 - odd
    potentials, odd, c, low_core, near_level = lax.optimization_barrier((potentials, odd, c, low_core, near_level))
    shape = jax.ShapeDtypeStruct
    bf16, f32 = jnp.bfloat16, jnp.float32
    both = ("space", "elec")

    def joint(pairs, cross):
        return [(2 * i + k, 2 * j + (k ^ cross)) for i, j in pairs for k in range(2)]

    piece = shape((rows, half), bf16)
    strip = shape((rows, 2 * LANES), bf16)
    near, far = call(
        keep_kernel,
        (piece,) * 2,
        [pl.BlockSpec(memory_space=pl.ANY)],
        "keep",
        scratch=[pltpu.VMEM((rows, layers, half), bf16), pltpu.SemaphoreType.DMA((4,))],
        moved=rows * cells * 4,
        limit=51,
    )(potentials)
    near_in_0 = lax.ppermute(near, both, joint(to_mate, 0))
    far_in_0 = lax.ppermute(far, both, joint(ahead, 0))
    near, far, potentials = lax.optimization_barrier((near, far, potentials))
    near_give, far_give, parcel, rim = call(
        give_kernel,
        (piece, piece, shape((rows, 2 * half + 2 * LANES), bf16), strip),
        [pl.BlockSpec(memory_space=pl.ANY)],
        "give",
        scratch=[pltpu.VMEM((rows, layers, 2 * half), bf16), pltpu.SemaphoreType.DMA((4,))],
        moved=rows * cells * 8,
        limit=47,
    )(potentials)
    parcel = lax.ppermute(parcel, "elec", swap)

    order = jnp.where(low_core, elec_order, jnp.concatenate([elec_order[rows:], elec_order[:rows]]))
    quadripoles, near_give = lax.optimization_barrier((quadripoles, near_give))
    weights = assemble(quadripoles, weighted_misfit, order)
    cross = call(cross_kernel, shape((rows, rows), bf16), [VMEM], "cross", moved=4 * rows * rows * 2)(weights)
    near_give, weights = lax.optimization_barrier((near_give, weights))
    far_give, cross = lax.optimization_barrier((far_give, cross))
    far_in_1 = lax.ppermute(far_give, both, joint(inner, 1))
    near_in_1 = lax.ppermute(near_give, both, joint(to_mate, 1))

    big = 2 * rows * rows * half * 2
    forms = call(
        plane_kernel,
        shape((2 * layers, half), f32),
        [VMEM] * 6,
        "plane",
        scratch=[pltpu.VMEM((2, 2 * rows, half), bf16)],
        limit=16,
        flops=big * 6,
        moved=rows * cells * 16,
    )(near, far, rim, parcel, weights, cross)

    bulk = 0.15 * salinity * water_content**cementation
    salt_scale = bulk / salinity
    water_scale = bulk * cementation / water_content
    row = lax.broadcasted_iota(jnp.int32, (layers, cells), 0)
    is_near = row == near_level
    is_mine = lax.broadcasted_iota(jnp.int32, (1, cells), 1) // half == c

    def spread(near_mine, near_other, far_mine, far_other):
        def line(mine, other):
            return jnp.where(is_mine, jnp.concatenate([mine, mine], 1), jnp.concatenate([other, other], 1))

        return jnp.where(is_near, line(near_mine, near_other), line(far_mine, far_other))

    forms_x = lax.ppermute(forms, "elec", swap)
    flat = anisotropy[1] * spread(forms[0:1], forms_x[0:1], forms[2:3], forms_x[2:3])
    flat = flat + anisotropy[2] * spread(forms[1:2], forms_x[1:2], forms[3:4], forms_x[3:4])
    salt_base, water_base = salt_scale * flat, water_scale * flat
    salt_scale, water_scale = salt_scale * anisotropy[0], water_scale * anisotropy[0]

    weights_e, forms = lax.optimization_barrier((weights, forms))
    carry_a, carry_b, early_a, early_b = call(
        early_kernel,
        (shape((rows, half), f32),) * 2 + (shape((8, half), f32),) * 2,
        [VMEM] * 5,
        "early",
        scratch=[pltpu.VMEM((rows, 2 * half), bf16)],
        flops=big * 4,
        moved=rows * cells * 16,
    )(far, near_in_0, far_in_0, weights_e, cross)
    early_a, salt_base, water_base, salt_scale, water_scale = lax.optimization_barrier(
        (early_a, salt_base, water_base, salt_scale, water_scale)
    )

    def close(name, start, masked, *given):
        return call(
            functools.partial(close_kernel, start=start, masked=masked), shape((1, half), f32), [VMEM] * 5, name, flops=big, moved=rows * cells * 8, limit=6
        )(*given)

    form_a = close("close_a", half, False, parcel, near_in_1, weights, carry_a, early_a)
    a_x = lax.ppermute(form_a, "elec", swap)
    far_in_1, form_a = lax.optimization_barrier((far_in_1, form_a))
    form_b = close("close_b", 0, True, far_in_1, near_in_1, weights, carry_b, early_b)
    b_same = lax.ppermute(form_b, both, joint(to_mate, 0))
    b_cross = lax.ppermute(form_b, both, joint(to_mate, 1))
    done = shape((layers, cells), f32)
    return pl.pallas_call(
        finish_kernel,
        out_shape=(done, done),
        in_specs=[VMEM] * 8,
        compiler_params=pltpu.CompilerParams(vmem_limit_bytes=2 * MIB),
        cost_estimate=pl.CostEstimate(flops=0, bytes_accessed=cells * 64, transcendentals=0),
        name="finish",
    )(b_same, b_cross, a_x, form_a, salt_scale, salt_base, water_scale, water_base)


def solution(mesh):
    split = P(("slab", "space"), None)
    placed = (P("elec", ("slab", "space"), None), P(), P(), P("slab"), split, split, split, P(None, ("slab", "space"), None))
    return jax.shard_map(local, mesh=mesh, in_specs=placed, out_specs=(split, split), check_vma=False)
```

```python
import functools
import jax
import jax.numpy as jnp
from jax import lax
from jax.experimental import pallas as pl
from jax.experimental.pallas import tpu as pltpu
from jax.sharding import PartitionSpec as P

NX = 32
LANES = 128
VMEM = pl.BlockSpec(memory_space=pltpu.VMEM)
MIB = 2**20


def call(kernel, outs, specs, name, scratch=(), limit=8, flops=0, moved=0):
    return pl.pallas_call(
        kernel,
        out_shape=outs,
        in_specs=specs,
        out_specs=jax.tree.map(lambda _: VMEM, outs),
        scratch_shapes=scratch,
        compiler_params=pltpu.CompilerParams(vmem_limit_bytes=limit * MIB),
        cost_estimate=pl.CostEstimate(flops=flops, bytes_accessed=moved, transcendentals=0),
        name=name,
    )


def dot(left, right):
    return jnp.dot(left, right, preferred_element_type=jnp.float32)


def spot():
    index = lax.axis_index("space")
    odd = lax.rem(index, 2)
    inside = jnp.where(odd == 1, index >= 2, index + 2 < lax.axis_size("space"))
    return odd, lax.axis_index("elec"), inside


def levels(block, odd):
    layers = jnp.swapaxes(block, 0, 1)
    return jnp.where(odd == 1, layers[0], layers[1]), jnp.where(odd == 1, layers[1], layers[0])


def keep_kernel(potentials, near, far, raw, sems):
    odd, core, _ = spot()
    rows, half = near.shape
    size = rows // sems.shape[0]
    cells = pl.ds(pl.multiple_of(core * half, LANES), half)
    copies = []
    for i in range(sems.shape[0]):
        part = pl.ds(i * size, size)
        copies.append(pltpu.make_async_copy(potentials.at[part, :, cells], raw.at[part], sems.at[i]))
        copies[-1].start()
    for i, copy in enumerate(copies):
        copy.wait()
        for k in range(2):

            @pl.when(odd == k)
            def _():
                for r in range(i * size, (i + 1) * size, 64):
                    layers = jnp.swapaxes(raw[r : r + 64], 0, 1)
                    near[r : r + 64, :], far[r : r + 64, :] = layers[1 - k], layers[k]


def give_kernel(potentials, near, far, parcel, rim, raw, sems):
    odd, core, _ = spot()
    rows, half = near.shape
    size = rows // sems.shape[0]
    copies = []
    for i in range(sems.shape[0]):
        part = pl.ds(i * size, size)
        copies.append(pltpu.make_async_copy(potentials.at[part], raw.at[part], sems.at[i]))
        copies[-1].start()
    for copy in copies:
        copy.wait()
    for k in range(2):
        low, high = slice(half - LANES, half), slice(half, half + LANES)
        inner, outer = (low, high) if k == 0 else (high, low)
        theirs = slice((1 - k) * half, (2 - k) * half)

        @pl.when(core == k)
        def _():
            for r in range(0, rows, 32):
                at = slice(r, r + 32)
                near_v, far_v = levels(raw[at], odd)
                near[at, :] = near_v[:, theirs]
                far[at, :] = far_v[:, theirs]
                parcel[at, :half] = near_v[:, theirs]
                parcel[at, half : 2 * half] = far_v[:, theirs]
                parcel[at, 2 * half : 2 * half + LANES] = near_v[:, inner]
                parcel[at, 2 * half + LANES :] = far_v[:, inner]
                rim[at, :LANES] = near_v[:, outer]
                rim[at, LANES:] = far_v[:, outer]


def cross_kernel(weights, out):
    n = out.shape[0]
    out[...] = (weights[n:, :n].astype(jnp.float32) + weights[:n, n:].astype(jnp.float32).T).astype(out.dtype)


def x_change(block):
    x = lax.rem(lax.broadcasted_iota(jnp.int32, block.shape, 1), NX)
    back = pltpu.roll(block, 2, 1)
    return jnp.where(x == 0, 0.0, block) - jnp.where(x == 1, 0.0, back)


def y_change(blocks, rim, first):
    lane = lax.broadcasted_iota(jnp.int32, rim.shape, 1)
    turned = [pltpu.roll(block, 2 * NX, 1) for block in blocks]
    above = jnp.where(first, rim, 0.0)
    below = jnp.where(first, 0.0, pltpu.roll(rim, 2 * NX, 1))
    out = []
    for b, block in enumerate(blocks):
        if b == 0:
            upper = jnp.where(lane < NX, above, block)
            lower = jnp.where(lane < NX, turned[-1], jnp.where(lane < 2 * NX, below, turned[0]))
        else:
            upper = block
            lower = jnp.where(lane < 2 * NX, turned[b - 1], turned[b])
        out.append(upper - lower)
    return out


def plane_kernel(near, far, rim, parcel, weights, cross, out, delta):
    first = spot()[1] == 0
    rows, half = near.shape
    count = half // LANES
    step = 128
    for layer, own in enumerate((near, far)):
        for group in range(2):
            for r in range(0, rows, step):
                at = pl.ds(r, step)
                if group == 0:
                    body = own[at, :]
                    edge = rim[at, layer * LANES : (layer + 1) * LANES]
                else:
                    body = parcel[at, layer * half : (layer + 1) * half]
                    edge = parcel[at, 2 * half + layer * LANES : 2 * half + (layer + 1) * LANES]
                body, edge = body.astype(jnp.float32), edge.astype(jnp.float32)
                blocks = [body[:, b * LANES : (b + 1) * LANES] for b in range(count)]
                along_y = y_change(blocks, edge, first)
                along_x = [x_change(block) for block in blocks]
                at = group * rows + r
                delta[0, at : at + step, :] = jnp.concatenate(along_y, axis=1).astype(jnp.bfloat16)
                delta[1, at : at + step, :] = jnp.concatenate(along_x, axis=1).astype(jnp.bfloat16)
        for part in range(2):
            total = jnp.zeros((8, half), jnp.float32)
            for at in range(0, 2 * rows, 256):
                grads = delta[part, at : at + 256, :]
                if at < rows:
                    mixed = dot(weights[at : at + 256, :rows], delta[part, :rows, :])
                else:
                    mixed = dot(weights[at : at + 256, rows:], delta[part, rows:, :])
                    mixed = mixed + dot(cross[at - rows : at - rows + 256, :], delta[part, :rows, :])
                total = total + jnp.sum((grads.astype(jnp.float32) * mixed).reshape(-1, 8, half), axis=0)
            total = 0.25 * jnp.sum(total, axis=0, keepdims=True)
            if part == 0:
                total = pltpu.roll(jnp.broadcast_to(total, (8, half)), half - NX, 1)
            else:
                total = jnp.broadcast_to(total, (8, half))
                total = jnp.concatenate(
                    [pltpu.roll(total[:, b * LANES : (b + 1) * LANES], LANES - 1, 1) for b in range(count)], axis=1
                )
            out[2 * layer + part : 2 * layer + part + 1, :] = total[:1]


def differences(inside, far, near_in, far_in, rows):
    near_v = near_in[rows, :].astype(jnp.float32)
    change_a = far[rows, :].astype(jnp.float32) - near_v
    change_b = jnp.where(inside, far_in[rows, :].astype(jnp.float32), 0.0) - near_v
    return change_a.astype(jnp.bfloat16), change_b.astype(jnp.bfloat16)


def early_kernel(far, near_in, far_in, weights, cross, carry_a, carry_b, out_a, out_b, delta):
    rows, half = far.shape
    inside = spot()[2]
    for r in range(0, rows, 128):
        at = pl.ds(r, 128)
        delta[at, :half], delta[at, half:] = differences(inside, far, near_in, far_in, at)
    total = jnp.zeros((8, 2 * half), jnp.float32)
    for r in range(0, rows, 256):
        mixed = dot(weights[r : r + 256, :rows], delta[...])
        carry = dot(cross[r : r + 256, :], delta[...])
        carry_a[r : r + 256, :] = carry[:, :half]
        carry_b[r : r + 256, :] = carry[:, half:]
        total = total + jnp.sum((delta[r : r + 256, :].astype(jnp.float32) * mixed).reshape(-1, 8, 2 * half), axis=0)
    out_a[...] = total[:, :half]
    out_b[...] = total[:, half:]


def close_kernel(upper, lower, weights, carry, early, out, start=0, masked=False):
    rows, half = lower.shape
    inside = spot()[2]
    wide = half // 2
    for c in range(0, half, wide):
        changes = []
        for r in range(0, rows, 128):
            above = upper[r : r + 128, start + c : start + c + wide]
            if masked:
                above = jnp.where(inside, above, jnp.zeros_like(above))
            changes.append(above - lower[r : r + 128, c : c + wide])
        delta = jnp.concatenate(changes, axis=0)
        mixed = carry[:, c : c + wide] + dot(weights[rows:, rows:], delta)
        total = early[:, c : c + wide] + jnp.sum((delta.astype(jnp.float32) * mixed).reshape(-1, 8, wide), axis=0)
        out[:, c : c + wide] = 0.25 * jnp.sum(total, axis=0, keepdims=True)


def finish_kernel(b, b_x, a_x, a, salt_scale, salt_base, water_scale, water_base, salt, water):
    odd, core, _ = spot()
    half = a.shape[1]
    for k in range(2):
        for n in range(2):

            @pl.when((odd == n) & (core == k))
            def _():
                for mine, other, row in ((a, a_x, 1 - n), (b, b_x, n)):
                    for value, side in ((mine, k), (other, 1 - k)):
                        at = (slice(row, row + 1), slice(side * half, (side + 1) * half))
                        salt[at] = salt_scale[at] * value[...] + salt_base[at]
                        water[at] = water_scale[at] * value[...] + water_base[at]


def assemble(quadripoles, weighted_misfit, order):
    left_side = (quadripoles[:, 0][None, :] == order[:, None]).astype(jnp.bfloat16) - (
        quadripoles[:, 1][None, :] == order[:, None]
    ).astype(jnp.bfloat16)
    third = quadripoles[:, 2][:, None] == order[None, :]
    fourth = quadripoles[:, 3][:, None] == order[None, :]
    signed = third.astype(jnp.float32) - fourth.astype(jnp.float32)
    right_side = (weighted_misfit.astype(jnp.float32)[:, None] * signed).astype(jnp.bfloat16)
    return dot(left_side, right_side).astype(jnp.bfloat16)


def local(potentials, elec_order, quadripoles, weighted_misfit, salinity, water_content, cementation, anisotropy):
    blocks = lax.axis_size("space")
    s = lax.axis_index("space")
    c = lax.axis_index("elec")
    rows, layers, cells = potentials.shape
    half = cells // 2
    odd = lax.rem(s, 2)
    to_mate = [(i, i ^ 1) for i in range(blocks)]
    ahead = [(i, (i + (2 if i % 2 else -2)) % blocks) for i in range(blocks)]
    inner = [(i, j) for i, j in ahead if abs(i - j) == 2]
    swap = [(0, 1), (1, 0)]
    low_core, near_level = c == 0, 1 - odd
    potentials, odd, c, low_core, near_level = lax.optimization_barrier((potentials, odd, c, low_core, near_level))
    shape = jax.ShapeDtypeStruct
    bf16, f32 = jnp.bfloat16, jnp.float32
    both = ("space", "elec")

    def joint(pairs, cross):
        return [(2 * i + k, 2 * j + (k ^ cross)) for i, j in pairs for k in range(2)]

    piece = shape((rows, half), bf16)
    strip = shape((rows, 2 * LANES), bf16)
    near, far = call(
        keep_kernel,
        (piece,) * 2,
        [pl.BlockSpec(memory_space=pl.ANY)],
        "keep",
        scratch=[pltpu.VMEM((rows, layers, half), bf16), pltpu.SemaphoreType.DMA((4,))],
        moved=rows * cells * 4,
        limit=51,
    )(potentials)
    near_in_0 = lax.ppermute(near, both, joint(to_mate, 0))
    far_in_0 = lax.ppermute(far, both, joint(ahead, 0))
    near, far, potentials = lax.optimization_barrier((near, far, potentials))
    near_give, far_give, parcel, rim = call(
        give_kernel,
        (piece, piece, shape((rows, 2 * half + 2 * LANES), bf16), strip),
        [pl.BlockSpec(memory_space=pl.ANY)],
        "give",
        scratch=[pltpu.VMEM((rows, layers, 2 * half), bf16), pltpu.SemaphoreType.DMA((4,))],
        moved=rows * cells * 8,
        limit=50,
    )(potentials)
    parcel = lax.ppermute(parcel, "elec", swap)

    order = jnp.where(low_core, elec_order, jnp.concatenate([elec_order[rows:], elec_order[:rows]]))
    quadripoles, near_give = lax.optimization_barrier((quadripoles, near_give))
    weights = assemble(quadripoles, weighted_misfit, order)
    cross = call(cross_kernel, shape((rows, rows), bf16), [VMEM], "cross", moved=4 * rows * rows * 2)(weights)
    far_in_1 = lax.ppermute(far_give, both, joint(inner, 1))
    near_in_1 = lax.ppermute(near_give, both, joint(to_mate, 1))

    big = 2 * rows * rows * half * 2
    forms = call(
        plane_kernel,
        shape((2 * layers, half), f32),
        [VMEM] * 6,
        "plane",
        scratch=[pltpu.VMEM((2, 2 * rows, half), bf16)],
        limit=16,
        flops=big * 6,
        moved=rows * cells * 16,
    )(near, far, rim, parcel, weights, cross)

    bulk = 0.15 * salinity * water_content**cementation
    salt_scale = bulk / salinity
    water_scale = bulk * cementation / water_content
    row = lax.broadcasted_iota(jnp.int32, (layers, cells), 0)
    is_near = row == near_level
    is_mine = lax.broadcasted_iota(jnp.int32, (1, cells), 1) // half == c

    def spread(near_mine, near_other, far_mine, far_other):
        def line(mine, other):
            return jnp.where(is_mine, jnp.concatenate([mine, mine], 1), jnp.concatenate([other, other], 1))

        return jnp.where(is_near, line(near_mine, near_other), line(far_mine, far_other))

    forms_x = lax.ppermute(forms, "elec", swap)
    flat = anisotropy[1] * spread(forms[0:1], forms_x[0:1], forms[2:3], forms_x[2:3])
    flat = flat + anisotropy[2] * spread(forms[1:2], forms_x[1:2], forms[3:4], forms_x[3:4])
    salt_base, water_base = salt_scale * flat, water_scale * flat
    salt_scale, water_scale = salt_scale * anisotropy[0], water_scale * anisotropy[0]

    weights_e, forms = lax.optimization_barrier((weights, forms))
    carry_a, carry_b, early_a, early_b = call(
        early_kernel,
        (shape((rows, half), f32),) * 2 + (shape((8, half), f32),) * 2,
        [VMEM] * 5,
        "early",
        scratch=[pltpu.VMEM((rows, 2 * half), bf16)],
        flops=big * 4,
        moved=rows * cells * 16,
    )(far, near_in_0, far_in_0, weights_e, cross)
    early_a, salt_base, water_base, salt_scale, water_scale = lax.optimization_barrier(
        (early_a, salt_base, water_base, salt_scale, water_scale)
    )

    def close(name, start, masked, *given):
        return call(
            functools.partial(close_kernel, start=start, masked=masked), shape((1, half), f32), [VMEM] * 5, name, flops=big, moved=rows * cells * 8, limit=6
        )(*given)

    form_a = close("close_a", half, False, parcel, near_in_1, weights, carry_a, early_a)
    a_x = lax.ppermute(form_a, "elec", swap)
    far_in_1, form_a = lax.optimization_barrier((far_in_1, form_a))
    form_b = close("close_b", 0, True, far_in_1, near_in_1, weights, carry_b, early_b)
    b_same = lax.ppermute(form_b, both, joint(to_mate, 0))
    b_cross = lax.ppermute(form_b, both, joint(to_mate, 1))
    done = shape((layers, cells), f32)
    return pl.pallas_call(
        finish_kernel,
        out_shape=(done, done),
        in_specs=[VMEM] * 8,
        compiler_params=pltpu.CompilerParams(vmem_limit_bytes=2 * MIB),
        cost_estimate=pl.CostEstimate(flops=0, bytes_accessed=cells * 64, transcendentals=0),
        name="finish",
    )(b_same, b_cross, a_x, form_a, salt_scale, salt_base, water_scale, water_base)


def solution(mesh):
    split = P(("slab", "space"), None)
    placed = (P("elec", ("slab", "space"), None), P(), P(), P("slab"), split, split, split, P(None, ("slab", "space"), None))
    return jax.shard_map(local, mesh=mesh, in_specs=placed, out_specs=(split, split), check_vma=False)
```
